1024 devices in a mesh: row: 128 (over z, y), rep: 8 (over x, core).
Axes of the slice: x: 4, y: 4, z: 32, core: 2. Of those that a mesh axis runs over, the one named last changes fastest.
Arguments:
- amplitudes: bfloat16 [128, 640, 640], P('row', None, 'rep'), may hold values from -6 to 6
- integrals: bfloat16 [4, 640, 8320], P(None, 'rep', 'row'), may hold values from -0.125 to 0.125
- occ_irrep: int32 [120], replicated, may hold values from 0 to 7
- virt_irrep: int32 [640], replicated, may hold values from 0 to 7, as said below
- slab_i: int32 [32], replicated, may hold values from 0 to 119
- slab_j: int32 [13], replicated, may hold values from 0 to 119
Outputs:
- cycle_term: bfloat16 [32, 640, 8320], P(None, 'row', 'rep')
The draws below stay inside these ranges and needn't reach their ends.
Inputs may be any that keep to these rules, and one draw needn't show every extreme that they name: virt_irrep never falls along the virtual orbitals; each of the 8 irreps forms one contiguous block of one or more orbitals.
All inputs are finite; a program needn't handle non-finite values.
Results may differ from the reference program's by a relative error of at most 0.017.
Values may be sent and summed in bfloat16 or wider, within the bound.
No kernel may reach another device: no remote copies, remote signals or barrier semaphores. Data moves between devices by JAX's collectives and lax.ppermute only.
A program may use at most 32 MiB of HBM per device.

```python
import jax
import jax.numpy as jnp
from jax import lax

V = 640
NOCC = 120
NK = 4
NJ = 13
NI = 32
PAIRS = 128
NJB = 8320
N_REP = 8


def draw_virt_irrep(key, part):
    key = jax.random.fold_in(key, 11)
    widths = jax.random.randint(key, (8,), 2, 6, dtype=jnp.int32)
    running = jnp.cumsum(widths).astype(jnp.int32)
    bounds = V * running // running[7]
    orbital = jnp.arange(V, dtype=jnp.int32)
    above = (orbital[:, None] >= bounds[None, :7]).astype(jnp.int32)
    return jnp.sum(above, axis=1).astype(jnp.int32)


def touch_ends(values, rng, low, largest):
    spot = [jax.random.randint(jax.random.fold_in(rng, axis), (), 0, length) for axis, length in enumerate(values.shape)]
    widest = values.shape.index(max(values.shape))
    beside = spot[:widest] + [(spot[widest] + 1) % values.shape[widest]] + spot[widest + 1:]
    return values.at[tuple(spot)].set(low).at[tuple(beside)].set(largest)


def block_scale(stream_key, extent, shards, low, top_value):
    gain, own = 1.0, jax.random.fold_in(stream_key, 6)
    for axis_at, blocks in shards:
        heights = jnp.exp(jax.random.uniform(jax.random.fold_in(own, axis_at), (blocks,), jnp.float32, low / len(shards), top_value / len(shards)))
        gain = gain * jnp.repeat(heights, extent[axis_at] // blocks).reshape([-1 if axis == axis_at else 1 for axis in range(len(extent))])
    return gain


def normal_values(rng, shape, spread, limit, pieces=(), kind=jnp.bfloat16):
    factor_of = block_scale(rng, shape, pieces, -0.22, 0.18) if pieces else 1.0
    drawn = jax.random.normal(rng, shape, jnp.float32) * spread * factor_of
    return jnp.minimum(jnp.maximum(drawn, -limit), limit).astype(kind)


def setup_inputs(seed: int = 0) -> dict:
    arg_keys = jax.random.split(jax.random.key(seed), 7)
    return {
        "amplitudes": normal_values(arg_keys[0], (PAIRS, V, V), 1.0, 6.0, ((0, 128), (2, 8))),
        "integrals": normal_values(arg_keys[1], (NK, V, NJB), (NK * V) ** -0.5, 0.125, ((1, 8), (2, 128))),
        "occ_irrep": touch_ends(jax.random.randint(arg_keys[2], (NOCC,), 0, 8), jax.random.fold_in(arg_keys[2], 1), 0, 7).astype(jnp.int32),
        "virt_irrep": draw_virt_irrep(jax.random.fold_in(arg_keys[6], 71), 0),
        "slab_i": touch_ends(jax.random.randint(arg_keys[4], (NI,), 0, NOCC), jax.random.fold_in(arg_keys[4], 1), 0, NOCC - 1).astype(jnp.int32),
        "slab_j": touch_ends(jax.random.randint(arg_keys[5], (NJ,), 0, NOCC), jax.random.fold_in(arg_keys[5], 1), 0, NOCC - 1).astype(jnp.int32),
    }


def reference(amplitudes, integrals, occ_irrep, virt_irrep, slab_i, slab_j):
    tiles = amplitudes.reshape(NI, NK, V, V)
    cblock = V // N_REP
    cycle = jnp.zeros((NI * V, NJB), jnp.float32)
    for block in range(N_REP):
        left = tiles[:, :, :, block * cblock:(block + 1) * cblock]
        left = left.transpose(0, 2, 1, 3).reshape(NI * V, NK * cblock)
        right = integrals[:, block * cblock:(block + 1) * cblock, :].reshape(NK * cblock, NJB)
        part = jnp.dot(left, right, preferred_element_type=jnp.float32).astype(jnp.bfloat16)
        part = lax.optimization_barrier(part)
        cycle = cycle + part.astype(jnp.float32)
    irr_rows = occ_irrep[slab_i]
    irr_cols = occ_irrep[slab_j]
    row_code = jnp.bitwise_xor(irr_rows[:, None], virt_irrep[None, :]).reshape(-1)
    col_code = jnp.bitwise_xor(irr_cols[:, None], virt_irrep[None, :]).reshape(-1)
    masked = jnp.where(row_code[:, None] == col_code[None, :], cycle, jnp.float32(0.0))
    return masked.astype(jnp.bfloat16).reshape(NI, V, NJB)
```

```python
import jax
import jax.numpy as jnp
from jax import lax
from jax.experimental import pallas as pl
from jax.experimental.pallas import tpu as pltpu
from jax.sharding import Mesh, PartitionSpec as P

BF16 = jnp.bfloat16
F32 = jnp.float32
LANES = 128
HALF = 64
SENT = 88
EXTRA = 16


def lookup(table, index):
    compare = index[:, None] == jnp.arange(table.shape[0], dtype=jnp.int32)[None, :]
    return jnp.sum(jnp.where(compare, table[None, :], 0), axis=1)


def dot(a, b, contract):
    return lax.dot_general(a, b, ((contract[:1], contract[1:]), ((), ())), preferred_element_type=F32)


def order_rows(gathered, shuffle, spread, pack, nk, pieces, ni, na):
    rows = gathered.shape[0] // nk
    depth = pack.shape[1]

    def kernel(g_ref, s_ref, t_ref, u_ref, o_ref):
        wide = []
        for k in range(nk):
            rowed = dot(s_ref[...], g_ref[k * rows : (k + 1) * rows, :], (1, 0)).astype(BF16)
            wide.append(dot(rowed, t_ref[...], (1, 0)).astype(BF16))
        for a in range(na):
            at = slice(a * LANES, (a + 1) * LANES)
            block = dot(jnp.concatenate([part[:, at] for part in wide], axis=1), u_ref[...], (1, 0))
            o_ref[:, a * ni : (a + 1) * ni, :] = block.astype(BF16).reshape(pieces, ni, depth)

    return pl.pallas_call(
        kernel,
        out_shape=jax.ShapeDtypeStruct((pieces, na * ni, depth), BF16),
        compiler_params=pltpu.CompilerParams(vmem_limit_bytes=32 << 20),
        name="order_rows",
    )(gathered, shuffle, spread, pack)


def multiply(a_own, a_other, b_own, b_other):
    pieces, rows, depth = a_own.shape
    nx = b_own.shape[0]

    def kernel(a0_ref, a1_ref, b0_ref, b1_ref, o_ref):
        a0, a1 = a0_ref[0], a1_ref[0]
        left = None
        for x in range(nx):
            total = None
            for a, b_ref in ((a0, b0_ref), (a1, b1_ref)):
                b = jnp.concatenate([b_ref[x, 0, :HALF, :], b_ref[x, 1, :HALF, :]], axis=0)
                part = dot(a, b, (1, 1))
                total = part if total is None else total + part
            o_ref[0, x, :rows, :] = total.astype(BF16)
        for a, b_ref in ((a0, b0_ref), (a1, b1_ref)):
            b = b_ref[0, 0, HALF:, :].astype(F32)
            for x in range(nx):
                for half in range(2):
                    if x + half:
                        b = b + b_ref[x, half, HALF:, :].astype(F32)
            part = dot(b.astype(BF16), a, (1, 1))
            left = part if left is None else left + part
        tail = jnp.concatenate([left[:8, LANES:], jnp.zeros((8, 2 * LANES - rows), F32)], axis=1)
        block = jnp.concatenate([left[:8, :LANES], tail], axis=0).astype(BF16)
        for x in range(nx):
            o_ref[0, x, rows:, :] = block

    a_spec = pl.BlockSpec((1, rows, depth), lambda p: (p, 0, 0))
    b_spec = pl.BlockSpec(b_own.shape, lambda p: (0, 0, 0, 0))
    return pl.pallas_call(
        kernel,
        grid=(pieces,),
        in_specs=[a_spec, a_spec, b_spec, b_spec],
        out_specs=pl.BlockSpec((1, nx, rows + EXTRA, LANES), lambda p: (p, 0, 0, 0)),
        out_shape=jax.ShapeDtypeStruct((pieces, nx, rows + EXTRA, LANES), BF16),
        compiler_params=pltpu.CompilerParams(vmem_limit_bytes=32 << 20),
        name="multiply",
    )(a_own, a_other, b_own, b_other)


def finish(parts, pick, row_code, col_code, q):
    pieces, nx, tall, _ = parts.shape
    rows = tall - EXTRA
    ncol = col_code.shape[1]

    def kernel(p_ref, pick_ref, r_ref, c_ref, o_ref, line):
        for p in range(pieces):
            total = p_ref[p, 0].astype(F32)
            for x in range(1, nx):
                total = total + p_ref[p, x].astype(F32)
            extra = total[rows:].astype(BF16)
            first = dot(extra, pick_ref[...], (0, 0))
            for half in range(2):
                at = (half * pieces + p) * q
                line[:, at : at + HALF] = total[:rows, half * HALF : (half + 1) * HALF]
                line[:LANES, at + HALF : at + q] = first[:, half : half + 1]
                line[LANES:, at + HALF : at + q] = first[: rows - LANES, 2 + half : 3 + half]
        kept = r_ref[...] == c_ref[...]
        o_ref[...] = jnp.where(kept, line[...], 0.0).astype(BF16)

    return pl.pallas_call(
        kernel,
        out_shape=jax.ShapeDtypeStruct((rows, ncol), BF16),
        scratch_shapes=[pltpu.VMEM((rows, ncol), F32)],
        compiler_params=pltpu.CompilerParams(vmem_limit_bytes=32 << 20),
        name="finish",
    )(parts, pick, row_code, col_code)


def iota(shape, axis):
    return lax.broadcasted_iota(jnp.int32, shape, axis)


def make_shards(nzh, nzl, ny, nx, nc):
    swap = [(s, 1 - s) for s in range(2)]

    def shards(amplitudes, integrals, occ_irrep, virt_irrep, slab_i, slab_j):
        vir, cblock = amplitudes.shape[1], amplitudes.shape[2]
        nk, q = integrals.shape[0], integrals.shape[2]
        ni = nzh * nzl
        pieces = nzl * ny
        na = vir // (nzh * pieces)
        zh, zl, y = lax.axis_index("zh"), lax.axis_index("zl"), lax.axis_index("y")
        x, c = lax.axis_index("x"), lax.axis_index("c")

        depth = -(-nk * cblock // LANES) * LANES
        w = integrals.transpose(2, 0, 1).reshape(q, nk * cblock)
        w = jnp.pad(w, ((0, 0), (0, depth - nk * cblock)))
        slot = (zh // 4) * 2 + zh % 2
        last = jnp.where(iota((SENT - HALF, 1), 0) == slot, w[HALF:], 0)
        w = jnp.concatenate([w[:HALF], last], axis=0)
        w = lax.all_gather(w, "zh", axis=0, tiled=True)

        t = amplitudes.reshape(vir // na, na * cblock)
        t = lax.all_to_all(t, "zh", 0, 0, tiled=True)
        t = lax.all_gather(t, "zl", axis=0, tiled=True)
        t = lax.all_gather(t, "y", axis=0, tiled=True)
        rows = ni * pieces
        to, at = iota((rows, rows), 0), iota((rows, rows), 1)
        piece, i = to // ni, to % ni
        shuffle = (at == (i % nzl) * (nzh * pieces) + (i // nzl) * pieces + piece).astype(BF16)
        at, to = iota((na * cblock, na * LANES), 0), iota((na * cblock, na * LANES), 1)
        spread = ((at // cblock == to // LANES) & (at % cblock == to % LANES)).astype(BF16)
        at, to = iota((nk * LANES, depth), 0), iota((nk * LANES, depth), 1)
        pack = ((at % LANES < cblock) & (to == (at // LANES) * cblock + at % LANES)).astype(BF16)
        t_own = order_rows(t, shuffle, spread, pack, nk, pieces, ni, na)
        t_other = lax.ppermute(t_own, "c", swap)

        w = w.reshape(nx, nc, 2, SENT, depth)[:, :, :, : HALF + EXTRA]
        w_own = lax.dynamic_index_in_dim(w, c, 1, keepdims=False)
        w_other = lax.ppermute(lax.dynamic_index_in_dim(w, 1 - c, 1, keepdims=False), "c", swap)

        parts = multiply(t_own, t_other, w_own, w_other)
        parts = parts.reshape(nx * pieces * parts.shape[2], LANES)
        parts = lax.all_to_all(parts, ("zl", "y", "x"), 0, 0, tiled=True)
        parts = parts.reshape(pieces, nx, -1, LANES)

        a_index = ((zh * nzl + zl) * ny + y) * na + jnp.arange(na, dtype=jnp.int32)
        irr_virt_rows = lookup(virt_irrep, a_index)
        irr_occ_rows = lookup(occ_irrep, slab_i)
        row_code = jnp.bitwise_xor(irr_virt_rows[:, None], irr_occ_rows[None, :]).reshape(na * ni, 1)
        ncol = 2 * pieces * q
        col_index = (x * nc + c) * ncol + jnp.arange(ncol, dtype=jnp.int32)
        irr_occ_cols = lookup(lookup(occ_irrep, slab_j), col_index // vir)
        irr_virt_cols = lookup(virt_irrep, col_index % vir)
        col_code = jnp.bitwise_xor(irr_occ_cols, irr_virt_cols)[None, :]
        row, col = iota((EXTRA, 4), 0), iota((EXTRA, 4), 1)
        pick = (row == (col // 2) * 8 + x * 2 + col % 2).astype(BF16)
        out = finish(parts, pick, row_code, col_code, q)
        return out.reshape(na, ni, ncol).transpose(1, 0, 2)

    return shards


def solution(mesh):
    nx, nc, ny = 4, 2, 4
    nzl = 2
    nzh = mesh.devices.size // (nx * nc * ny * nzl)
    fine = Mesh(mesh.devices.reshape(nzh, nzl, ny, nx, nc), ("zh", "zl", "y", "x", "c"))
    row, rep = ("zh", "zl", "y"), ("x", "c")
    return jax.shard_map(
        make_shards(nzh, nzl, ny, nx, nc),
        mesh=fine,
        in_specs=(P(row, None, rep), P(None, rep, row), P(), P(), P(), P()),
        out_specs=P(None, row, rep),
        check_vma=False,
    )
```

```python
import jax
import jax.numpy as jnp
from jax import lax
from jax.experimental import pallas as pl
from jax.experimental.pallas import tpu as pltpu
from jax.sharding import Mesh, PartitionSpec as P

BF16 = jnp.bfloat16
F32 = jnp.float32
LANES = 128
HALF = 64
SENT = 72
EXTRA = 16


def lookup(table, index):
    compare = index[:, None] == jnp.arange(table.shape[0], dtype=jnp.int32)[None, :]
    return jnp.sum(jnp.where(compare, table[None, :], 0), axis=1)


def dot(a, b, contract):
    return lax.dot_general(a, b, ((contract[:1], contract[1:]), ((), ())), preferred_element_type=F32)


def order_rows(gathered, shuffle, spread, pack, nk, pieces, ni, na):
    rows = gathered.shape[0] // nk
    depth = pack.shape[1]

    def kernel(g_ref, s_ref, t_ref, u_ref, o_ref):
        wide = []
        for k in range(nk):
            rowed = dot(s_ref[...], g_ref[k * rows : (k + 1) * rows, :], (1, 0)).astype(BF16)
            wide.append(dot(rowed, t_ref[...], (1, 0)).astype(BF16))
        for a in range(na):
            at = slice(a * LANES, (a + 1) * LANES)
            block = dot(jnp.concatenate([part[:, at] for part in wide], axis=1), u_ref[...], (1, 0))
            o_ref[:, a * ni : (a + 1) * ni, :] = block.astype(BF16).reshape(pieces, ni, depth)

    return pl.pallas_call(
        kernel,
        out_shape=jax.ShapeDtypeStruct((pieces, na * ni, depth), BF16),
        compiler_params=pltpu.CompilerParams(vmem_limit_bytes=32 << 20),
        name="order_rows",
    )(gathered, shuffle, spread, pack)


def multiply(place, a_own, a_other, sets):
    pieces, rows, depth = a_own.shape
    nx, tall = sets[0].shape[:2]

    def kernel(place_ref, a0_ref, a1_ref, s0, s1, s2, s3, o_ref, main, tail):
        @pl.when(pl.program_id(0) == 0)
        def _():
            tail[...] = jnp.zeros_like(tail)
            for d, s_ref in enumerate((s0, s1, s2, s3)):
                other, half, first = place_ref[d, 0], place_ref[d, 1], place_ref[d, 2]
                total = tail[other]
                for j in range(nx):
                    main[other, lax.rem(first + j, nx), half] = s_ref[j, :HALF, :]
                    total = total + s_ref[j, HALF:, :].astype(F32)
                tail[other] = total

        left = None
        for x in range(nx):
            total = None
            for at, a_ref in enumerate((a0_ref, a1_ref)):
                part = dot(a_ref[0], main[at, x].reshape(2 * HALF, depth), (1, 1))
                total = part if total is None else total + part
            o_ref[0, x, :rows, :] = total.astype(BF16)
        for at, a_ref in enumerate((a0_ref, a1_ref)):
            part = dot(tail[at].astype(BF16), a_ref[0], (1, 1))
            left = part if left is None else left + part
        end = jnp.concatenate([left[:, LANES:], jnp.zeros((tall - HALF, 2 * LANES - rows), F32)], axis=1)
        block = jnp.concatenate([left[:, :LANES], end], axis=0).astype(BF16)
        for x in range(nx):
            o_ref[0, x, rows:, :] = block

    a_spec = pl.BlockSpec((1, rows, depth), lambda p, place: (p, 0, 0))
    s_spec = pl.BlockSpec((nx, tall, depth), lambda p, place: (0, 0, 0))
    return pl.pallas_call(
        kernel,
        grid_spec=pltpu.PrefetchScalarGridSpec(
            num_scalar_prefetch=1,
            grid=(pieces,),
            in_specs=[a_spec, a_spec] + [s_spec] * 4,
            out_specs=pl.BlockSpec((1, nx, rows + EXTRA, LANES), lambda p, place: (p, 0, 0, 0)),
            scratch_shapes=[
                pltpu.VMEM((2, nx, 2, HALF, depth), BF16),
                pltpu.VMEM((2, tall - HALF, depth), F32),
            ],
        ),
        out_shape=jax.ShapeDtypeStruct((pieces, nx, rows + EXTRA, LANES), BF16),
        compiler_params=pltpu.CompilerParams(vmem_limit_bytes=32 << 20),
        name="multiply",
    )(place, a_own, a_other, *sets)


def finish(parts, pick, row_code, col_code, q):
    pieces, nx, tall, _ = parts.shape
    rows = tall - EXTRA
    ncol = col_code.shape[1]

    def kernel(p_ref, pick_ref, r_ref, c_ref, o_ref, line):
        for p in range(pieces):
            total = p_ref[p, 0].astype(F32)
            for x in range(1, nx):
                total = total + p_ref[p, x].astype(F32)
            extra = total[rows:].astype(BF16)
            first = dot(extra, pick_ref[...], (0, 0))
            for half in range(2):
                at = (half * pieces + p) * q
                line[:, at : at + HALF] = total[:rows, half * HALF : (half + 1) * HALF]
                line[:LANES, at + HALF : at + q] = first[:, half : half + 1]
                line[LANES:, at + HALF : at + q] = first[: rows - LANES, 2 + half : 3 + half]
        kept = r_ref[...] == c_ref[...]
        o_ref[...] = jnp.where(kept, line[...], 0.0).astype(BF16)

    return pl.pallas_call(
        kernel,
        out_shape=jax.ShapeDtypeStruct((rows, ncol), BF16),
        scratch_shapes=[pltpu.VMEM((rows, ncol), F32)],
        compiler_params=pltpu.CompilerParams(vmem_limit_bytes=32 << 20),
        name="finish",
    )(parts, pick, row_code, col_code)


def iota(shape, axis):
    return lax.broadcasted_iota(jnp.int32, shape, axis)


def make_shards(nzh, nzl, ny, nx, nc):
    swap = [(s, 1 - s) for s in range(2)]

    def shards(amplitudes, integrals, occ_irrep, virt_irrep, slab_i, slab_j):
        vir, cblock = amplitudes.shape[1], amplitudes.shape[2]
        nk, q = integrals.shape[0], integrals.shape[2]
        ni = nzh * nzl
        pieces = nzl * ny
        na = vir // (nzh * pieces)
        zh, zl, y = lax.axis_index("zh"), lax.axis_index("zl"), lax.axis_index("y")
        x, c = lax.axis_index("x"), lax.axis_index("c")

        depth = -(-nk * cblock // LANES) * LANES
        w = integrals.transpose(2, 0, 1).reshape(q, nk * cblock)
        w = jnp.pad(w, ((0, 0), (0, depth - nk * cblock)))
        slot = (zh // 4) * 2 + zh % 2
        last = jnp.where(iota((SENT - HALF, 1), 0) == slot, w[HALF:], 0)
        w = jnp.concatenate([w[:HALF], last], axis=0)
        hop = lambda by: [(s, (s - by) % nzh) for s in range(nzh)]
        t = amplitudes.reshape(vir // na, na * cblock)
        t = lax.all_to_all(t, "zh", 0, 0, tiled=True)
        w = [w] + [lax.ppermute(w, "zh", hop(4 * j)) for j in range(1, nx)]
        t, w = lax.optimization_barrier((t, w))
        w = jnp.stack(w)
        sets, place = [], []
        near = (0, 1, 2, -1)
        for d in range(4):
            moves = []
            for s in range(nzh):
                for sc in range(nc):
                    to = (s + near[(d + 2 * sc) % 4]) % nzh
                    moves.append((s * nc + sc, to * nc + (s // 2) % 2))
            sets.append(lax.ppermute(w, ("zh", "c"), moves))
            offset = (zh - d) % 4
            came_c = jnp.where(offset // 2 == c, 0, 1)
            step = jnp.array(near, jnp.int32)[(d + 2 * came_c) % 4]
            place.append(jnp.stack([jnp.where(came_c == c, 0, 1), offset % 2, (zh - step) % nzh // 4]))
        place = jnp.stack(place).astype(jnp.int32)
        t = lax.all_gather(t, "zl", axis=0, tiled=True)
        t = lax.all_gather(t, "y", axis=0, tiled=True)
        t, sets[:3] = lax.optimization_barrier((t, sets[:3]))
        rows = ni * pieces
        to, at = iota((rows, rows), 0), iota((rows, rows), 1)
        piece, i = to // ni, to % ni
        shuffle = (at == (i % nzl) * (nzh * pieces) + (i // nzl) * pieces + piece).astype(BF16)
        at, to = iota((na * cblock, na * LANES), 0), iota((na * cblock, na * LANES), 1)
        spread = ((at // cblock == to // LANES) & (at % cblock == to % LANES)).astype(BF16)
        at, to = iota((nk * LANES, depth), 0), iota((nk * LANES, depth), 1)
        pack = ((at % LANES < cblock) & (to == (at // LANES) * cblock + at % LANES)).astype(BF16)
        t_own = order_rows(t, shuffle, spread, pack, nk, pieces, ni, na)
        t_other = lax.ppermute(t_own, "c", swap)

        parts = multiply(place, t_own, t_other, sets)
        parts = parts.reshape(nx * pieces * parts.shape[2], LANES)
        parts = lax.all_to_all(parts, ("zl", "y", "x"), 0, 0, tiled=True)
        parts = parts.reshape(pieces, nx, -1, LANES)

        a_index = ((zh * nzl + zl) * ny + y) * na + jnp.arange(na, dtype=jnp.int32)
        irr_virt_rows = lookup(virt_irrep, a_index)
        irr_occ_rows = lookup(occ_irrep, slab_i)
        row_code = jnp.bitwise_xor(irr_virt_rows[:, None], irr_occ_rows[None, :]).reshape(na * ni, 1)
        ncol = 2 * pieces * q
        col_index = (x * nc + c) * ncol + jnp.arange(ncol, dtype=jnp.int32)
        irr_occ_cols = lookup(lookup(occ_irrep, slab_j), col_index // vir)
        irr_virt_cols = lookup(virt_irrep, col_index % vir)
        col_code = jnp.bitwise_xor(irr_occ_cols, irr_virt_cols)[None, :]
        row, col = iota((EXTRA, 4), 0), iota((EXTRA, 4), 1)
        pick = (row == (col // 2) * 8 + x * 2 + col % 2).astype(BF16)
        out = finish(parts, pick, row_code, col_code, q)
        return out.reshape(na, ni, ncol).transpose(1, 0, 2)

    return shards


def solution(mesh):
    nx, nc, ny = 4, 2, 4
    nzl = 2
    nzh = mesh.devices.size // (nx * nc * ny * nzl)
    fine = Mesh(mesh.devices.reshape(nzh, nzl, ny, nx, nc), ("zh", "zl", "y", "x", "c"))
    row, rep = ("zh", "zl", "y"), ("x", "c")
    return jax.shard_map(
        make_shards(nzh, nzl, ny, nx, nc),
        mesh=fine,
        in_specs=(P(row, None, rep), P(None, rep, row), P(), P(), P(), P()),
        out_specs=P(None, row, rep),
        check_vma=False,
    )
```

```python
import jax
import jax.numpy as jnp
from jax import lax
from jax.experimental import pallas as pl
from jax.experimental.pallas import tpu as pltpu
from jax.sharding import Mesh, PartitionSpec as P

BF16 = jnp.bfloat16
F32 = jnp.float32
LANES = 128
HALF = 64
SENT = 72
EXTRA = 16


def lookup(table, index):
    compare = index[:, None] == jnp.arange(table.shape[0], dtype=jnp.int32)[None, :]
    return jnp.sum(jnp.where(compare, table[None, :], 0), axis=1)


def dot(a, b, contract):
    return lax.dot_general(a, b, ((contract[:1], contract[1:]), ((), ())), preferred_element_type=F32)


def order_rows(gathered, shuffle, spread, pack, nk, pieces, ni, na):
    rows = gathered.shape[0] // nk
    depth = pack.shape[1]

    def kernel(g_ref, s_ref, t_ref, u_ref, o_ref):
        wide = []
        for k in range(nk):
            rowed = dot(s_ref[...], g_ref[k * rows : (k + 1) * rows, :], (1, 0)).astype(BF16)
            wide.append(dot(rowed, t_ref[...], (1, 0)).astype(BF16))
        for a in range(na):
            at = slice(a * LANES, (a + 1) * LANES)
            block = dot(jnp.concatenate([part[:, at] for part in wide], axis=1), u_ref[...], (1, 0))
            o_ref[:, a * ni : (a + 1) * ni, :] = block.astype(BF16).reshape(pieces, ni, depth)

    return pl.pallas_call(
        kernel,
        out_shape=jax.ShapeDtypeStruct((pieces, na * ni, depth), BF16),
        compiler_params=pltpu.CompilerParams(vmem_limit_bytes=32 << 20),
        name="order_rows",
    )(gathered, shuffle, spread, pack)


def multiply(a_own, a_other, b_own, b_other):
    pieces, rows, depth = a_own.shape
    nx, tiles, tall = b_own.shape[1:4]
    step = 2
    wide = (nx + 1) * LANES

    def kernel(a0_ref, a1_ref, b0_ref, b1_ref, o_ref, cols):
        @pl.when(pl.program_id(0) == 0)
        def _():
            for at, b_ref in enumerate((b0_ref, b1_ref)):
                for tile in range(tiles):
                    spot = slice(at * depth + tile * LANES, at * depth + (tile + 1) * LANES)
                    total = jnp.zeros((tall - HALF, LANES), F32)
                    for x in range(nx):
                        block = jnp.concatenate([b_ref[0, x, tile, :HALF, :], b_ref[1, x, tile, :HALF, :]], axis=0)
                        cols[spot, x * LANES : (x + 1) * LANES] = block.T
                        for half in range(2):
                            total = total + b_ref[half, x, tile, HALF:, :].astype(F32)
                    total = jnp.concatenate([total, jnp.zeros((LANES - total.shape[0], LANES), F32)], axis=0)
                    cols[spot, nx * LANES :] = total.astype(BF16).T

        a = jnp.concatenate([a0_ref[...].reshape(step * rows, depth), a1_ref[...].reshape(step * rows, depth)], axis=1)
        out = dot(a, cols[...], (1, 0))
        for p in range(step):
            own = out[p * rows : (p + 1) * rows]
            left = own[:, nx * LANES :].T[: tall - HALF]
            end = jnp.concatenate([left[:, LANES:], jnp.zeros((tall - HALF, 2 * LANES - rows), F32)], axis=1)
            block = jnp.concatenate([left[:, :LANES], end], axis=0).astype(BF16)
            for x in range(nx):
                o_ref[p, x, :rows, :] = own[:, x * LANES : (x + 1) * LANES].astype(BF16)
                o_ref[p, x, rows:, :] = block

    a_spec = pl.BlockSpec((step, rows, depth), lambda p: (p, 0, 0))
    b_spec = pl.BlockSpec(b_own.shape, lambda p: (0, 0, 0, 0, 0))
    return pl.pallas_call(
        kernel,
        grid=(pieces // step,),
        in_specs=[a_spec, a_spec, b_spec, b_spec],
        out_specs=pl.BlockSpec((step, nx, rows + EXTRA, LANES), lambda p: (p, 0, 0, 0)),
        out_shape=jax.ShapeDtypeStruct((pieces, nx, rows + EXTRA, LANES), BF16),
        scratch_shapes=[pltpu.VMEM((2 * depth, wide), BF16)],
        compiler_params=pltpu.CompilerParams(vmem_limit_bytes=32 << 20),
        name="multiply",
    )(a_own, a_other, b_own, b_other)


def finish(parts, pick, row_code, col_code, q):
    pieces, nx, tall, _ = parts.shape
    rows = tall - EXTRA
    ncol = col_code.shape[1]

    def kernel(p_ref, pick_ref, r_ref, c_ref, o_ref, line):
        for p in range(pieces):
            total = p_ref[p, 0].astype(F32)
            for x in range(1, nx):
                total = total + p_ref[p, x].astype(F32)
            extra = total[rows:].astype(BF16)
            first = dot(extra, pick_ref[...], (0, 0))
            for half in range(2):
                at = (half * pieces + p) * q
                line[:, at : at + HALF] = total[:rows, half * HALF : (half + 1) * HALF]
                line[:LANES, at + HALF : at + q] = first[:, half : half + 1]
                line[LANES:, at + HALF : at + q] = first[: rows - LANES, 2 + half : 3 + half]
        kept = r_ref[...] == c_ref[...]
        o_ref[...] = jnp.where(kept, line[...], 0.0).astype(BF16)

    return pl.pallas_call(
        kernel,
        out_shape=jax.ShapeDtypeStruct((rows, ncol), BF16),
        scratch_shapes=[pltpu.VMEM((rows, ncol), F32)],
        compiler_params=pltpu.CompilerParams(vmem_limit_bytes=32 << 20),
        name="finish",
    )(parts, pick, row_code, col_code)


def iota(shape, axis):
    return lax.broadcasted_iota(jnp.int32, shape, axis)


def make_shards(nzl, ny, nx, nc):
    nzh = nx * 2 * nc
    swap = [(s, 1 - s) for s in range(2)]

    def shards(amplitudes, integrals, occ_irrep, virt_irrep, slab_i, slab_j):
        vir, cblock = amplitudes.shape[1], amplitudes.shape[2]
        nk, q = integrals.shape[0], integrals.shape[2]
        ni = nzh * nzl
        pieces = nzl * ny
        na = vir // (nzh * pieces)
        zh = lax.axis_index("zg") * 2 * nc + lax.axis_index("zm")
        zl, y = lax.axis_index("zl"), lax.axis_index("y")
        x, c = lax.axis_index("x"), lax.axis_index("c")

        depth = -(-nk * cblock // LANES) * LANES
        w = integrals.transpose(2, 0, 1).reshape(q, nk * cblock)
        w = jnp.pad(w, ((0, 0), (0, depth - nk * cblock)))
        slot = lax.axis_index("zg") * 2 + zh % 2
        last = jnp.where(iota((SENT - HALF, 1), 0) == slot, w[HALF:], 0)
        w = jnp.concatenate([w[:HALF], last], axis=0)
        t = amplitudes.reshape(nx, -1, na * cblock)
        width = -(-na * cblock // LANES) * LANES
        t = jnp.pad(t, ((0, 0), (0, 0), (0, width - na * cblock)))
        parts = [t[:, :, at : at + LANES] for at in range(0, width, LANES)]
        parts += [jnp.broadcast_to(w[:, at : at + LANES], (nx, SENT, LANES)) for at in range(0, depth, LANES)]
        both = lax.all_to_all(jnp.concatenate(parts, axis=1), "zg", 0, 0)
        height = t.shape[1]
        t = jnp.concatenate([both[:, at * height : (at + 1) * height] for at in range(width // LANES)], axis=2)
        t = t[:, :, : na * cblock].reshape(nx, 2 * nc, pieces, na * cblock).transpose(1, 0, 2, 3)
        w = both[:, width // LANES * height :].reshape(nx, depth // LANES, SENT, LANES)
        t = lax.all_to_all(t.reshape(nzh * pieces, na * cblock), "zm", 0, 0, tiled=True)
        t, w = lax.optimization_barrier((t, w))
        w = lax.all_to_all(jnp.broadcast_to(w, (2 * nc, *w.shape)), "zm", 0, 0)
        t = lax.all_gather(t, "zl", axis=0, tiled=True)
        t = lax.all_gather(t, "y", axis=0, tiled=True)
        t, w = lax.optimization_barrier((t, w))
        w = w.reshape(nc, 2, *w.shape[1:])
        w_own = lax.dynamic_index_in_dim(w, c, 0, keepdims=False)
        w_other = lax.ppermute(lax.dynamic_index_in_dim(w, 1 - c, 0, keepdims=False), "c", swap)
        rows = ni * pieces
        to, at = iota((rows, rows), 0), iota((rows, rows), 1)
        piece, i = to // ni, to % ni
        swapped = i // nzl % (2 * nc) * nx + i // nzl // (2 * nc)
        shuffle = (at == (i % nzl) * (nzh * pieces) + swapped * pieces + piece).astype(BF16)
        at, to = iota((na * cblock, na * LANES), 0), iota((na * cblock, na * LANES), 1)
        spread = ((at // cblock == to // LANES) & (at % cblock == to % LANES)).astype(BF16)
        at, to = iota((nk * LANES, depth), 0), iota((nk * LANES, depth), 1)
        pack = ((at % LANES < cblock) & (to == (at // LANES) * cblock + at % LANES)).astype(BF16)
        t_own = order_rows(t, shuffle, spread, pack, nk, pieces, ni, na)
        t_other = lax.ppermute(t_own, "c", swap)

        parts = multiply(t_own, t_other, w_own, w_other)
        parts = parts.reshape(nx * pieces * parts.shape[2], LANES)
        parts = lax.all_to_all(parts, ("zl", "y", "x"), 0, 0, tiled=True)
        parts = parts.reshape(pieces, nx, -1, LANES)

        a_index = ((zh * nzl + zl) * ny + y) * na + jnp.arange(na, dtype=jnp.int32)
        irr_virt_rows = lookup(virt_irrep, a_index)
        irr_occ_rows = lookup(occ_irrep, slab_i)
        row_code = jnp.bitwise_xor(irr_virt_rows[:, None], irr_occ_rows[None, :]).reshape(na * ni, 1)
        ncol = 2 * pieces * q
        col_index = (x * nc + c) * ncol + jnp.arange(ncol, dtype=jnp.int32)
        irr_occ_cols = lookup(lookup(occ_irrep, slab_j), col_index // vir)
        irr_virt_cols = lookup(virt_irrep, col_index % vir)
        col_code = jnp.bitwise_xor(irr_occ_cols, irr_virt_cols)[None, :]
        row, col = iota((EXTRA, 4), 0), iota((EXTRA, 4), 1)
        pick = (row == (col // 2) * 8 + x * 2 + col % 2).astype(BF16)
        out = finish(parts, pick, row_code, col_code, q)
        return out.reshape(na, ni, ncol).transpose(1, 0, 2)

    return shards


def solution(mesh):
    nx, nc, ny = 4, 2, 4
    nzl = 2
    fine = Mesh(mesh.devices.reshape(nx, 2 * nc, nzl, ny, nx, nc), ("zg", "zm", "zl", "y", "x", "c"))
    row, rep = ("zg", "zm", "zl", "y"), ("x", "c")
    return jax.shard_map(
        make_shards(nzl, ny, nx, nc),
        mesh=fine,
        in_specs=(P(row, None, rep), P(None, rep, row), P(), P(), P(), P()),
        out_specs=P(None, row, rep),
        check_vma=False,
    )
```

```python
import jax
import jax.numpy as jnp
import numpy as np
from jax import lax
from jax.experimental import pallas as pl
from jax.experimental.pallas import tpu as pltpu
from jax.sharding import Mesh, PartitionSpec as P

BF16 = jnp.bfloat16
F32 = jnp.float32
LANES = 128
HALF = 64
SENT = 72
EXTRA = 16


def lookup(table, index):
    compare = index[:, None] == jnp.arange(table.shape[0], dtype=jnp.int32)[None, :]
    return jnp.sum(jnp.where(compare, table[None, :], 0), axis=1)


def dot(a, b, contract):
    return lax.dot_general(a, b, ((contract[:1], contract[1:]), ((), ())), preferred_element_type=F32)


def onehot(hit):
    return np.asarray(hit).astype(np.dtype(jnp.bfloat16))


def order_rows(gathered, nk, pieces, ni, na, cblock, depth):
    rows = ni * pieces
    to, at = np.indices((rows, rows))
    shuffle = onehot(at == to % ni * pieces + to // ni)
    at, to = np.indices((na * cblock, na * LANES))
    spread = onehot((at // cblock == to // LANES) & (at % cblock == to % LANES))
    at, to = np.indices((nk * LANES, depth))
    pack = onehot((at % LANES < cblock) & (to == at // LANES * cblock + at % LANES))

    def kernel(g_ref, s_ref, t_ref, u_ref, o_ref):
        wide = []
        for k in range(nk):
            rowed = dot(s_ref[...], g_ref[k * rows : (k + 1) * rows, :], (1, 0)).astype(BF16)
            wide.append(dot(rowed, t_ref[...], (1, 0)).astype(BF16))
        for a in range(na):
            at = slice(a * LANES, (a + 1) * LANES)
            block = dot(jnp.concatenate([part[:, at] for part in wide], axis=1), u_ref[...], (1, 0))
            o_ref[:, a * ni : (a + 1) * ni, :] = block.astype(BF16).reshape(pieces, ni, depth)

    return pl.pallas_call(
        kernel,
        out_shape=jax.ShapeDtypeStruct((pieces, na * ni, depth), BF16),
        compiler_params=pltpu.CompilerParams(vmem_limit_bytes=32 << 20),
        name="order_rows",
    )(gathered, jnp.asarray(shuffle), jnp.asarray(spread), jnp.asarray(pack))


def multiply(zl, a_own, a_other, blocks):
    pieces, rows, depth = a_own.shape
    nx, halves, tall, _ = blocks[0].shape
    step = min(2, pieces)
    to, at = np.indices((nx * EXTRA, 4 * (tall - HALF)))
    x, part, parity, half = to // EXTRA, to % EXTRA // 4, to % 4 // 2, to % 2
    pick = onehot((to % EXTRA < 8) & (at == (part * 2 + parity) * (tall - HALF) + x * halves + half))

    def kernel(zl_ref, a0_ref, a1_ref, b0, b1, b2, b3, pick_ref, o_ref, cols):
        @pl.when(pl.program_id(0) == 0)
        def _():
            for n, b_ref in enumerate((b0, b1, b2, b3)):
                parity = zl_ref[0] if n < 2 else 1 - zl_ref[0]
                spot = slice(n % 2 * depth, (n % 2 + 1) * depth)
                total = jnp.zeros((tall - HALF, depth), F32)
                for x in range(nx):
                    block = jnp.concatenate([b_ref[x, half, :HALF, :] for half in range(halves)], axis=0)
                    lane = pl.multiple_of((x * 2 + parity) * LANES, LANES)
                    cols[spot, pl.ds(lane, LANES)] = block.T
                    for half in range(halves):
                        total = total + b_ref[x, half, HALF:, :].astype(F32)
                total = jnp.concatenate([total, jnp.zeros((LANES - total.shape[0], depth), F32)], axis=0)
                lane = pl.multiple_of((nx * 2 + parity) * LANES, LANES)
                cols[spot, pl.ds(lane, LANES)] = total.astype(BF16).T

        a = jnp.concatenate([a0_ref[...].reshape(step * rows, depth), a1_ref[...].reshape(step * rows, depth)], axis=1)
        out = dot(a, cols[...], (1, 0))
        for p in range(step):
            own = out[p * rows : (p + 1) * rows]
            left = [own[:, at * LANES : (at + 1) * LANES].T[: tall - HALF] for at in (nx * 2, nx * 2 + 1)]
            blank = jnp.zeros((tall - HALF, 2 * LANES - rows), F32)
            left = [part[:, :LANES] for part in left] + [jnp.concatenate([part[:, LANES:], blank], axis=1) for part in left]
            left = dot(pick_ref[...], jnp.concatenate(left, axis=0).astype(BF16), (1, 0)).astype(BF16)
            for x in range(nx):
                for parity in range(2):
                    at = (x * 2 + parity) * LANES
                    o_ref[p, x, parity * rows : (parity + 1) * rows, :] = own[:, at : at + LANES].astype(BF16)
                o_ref[p, x, 2 * rows :, :] = left[x * EXTRA : (x + 1) * EXTRA]

    a_spec = pl.BlockSpec((step, rows, depth), lambda p, zl: (p, 0, 0))
    b_spec = pl.BlockSpec(blocks[0].shape, lambda p, zl: (0, 0, 0, 0))
    return pl.pallas_call(
        kernel,
        grid_spec=pltpu.PrefetchScalarGridSpec(
            num_scalar_prefetch=1,
            grid=(pieces // step,),
            in_specs=[a_spec, a_spec] + [b_spec] * 4 + [pl.BlockSpec(pick.shape, lambda p, zl: (0, 0))],
            out_specs=pl.BlockSpec((step, nx, 2 * rows + EXTRA, LANES), lambda p, zl: (p, 0, 0, 0)),
            scratch_shapes=[pltpu.VMEM((2 * depth, (nx + 1) * 2 * LANES), BF16)],
        ),
        out_shape=jax.ShapeDtypeStruct((pieces, nx, 2 * rows + EXTRA, LANES), BF16),
        compiler_params=pltpu.CompilerParams(vmem_limit_bytes=32 << 20),
        name="multiply",
    )(zl, a_own, a_other, *blocks, jnp.asarray(pick))


def finish(parts, row_code, col_code, q):
    pieces, nx, tall, _ = parts.shape
    rows = (tall - EXTRA) // 2
    ncol = col_code.shape[1]
    at, to = np.indices((EXTRA, 8))
    turn = onehot(at == to)

    def kernel(p_ref, turn_ref, r_ref, c_ref, o_ref, line):
        for p in range(pieces):
            total = p_ref[p, 0].astype(F32)
            for x in range(1, nx):
                total = total + p_ref[p, x].astype(F32)
            last = dot(total[2 * rows :].astype(BF16), turn_ref[...], (0, 0))
            for parity in range(2):
                for half in range(2):
                    at = ((half * 2 + parity) * pieces + p) * q
                    own = slice(parity * rows, (parity + 1) * rows)
                    line[:, at : at + HALF] = total[own, half * HALF : (half + 1) * HALF]
                    col = parity * 2 + half
                    line[:LANES, at + HALF : at + q] = last[:, col : col + 1]
                    line[LANES:, at + HALF : at + q] = last[: rows - LANES, 4 + col : 5 + col]
        kept = r_ref[...] == c_ref[...]
        o_ref[...] = jnp.where(kept, line[...], 0.0).astype(BF16)

    return pl.pallas_call(
        kernel,
        out_shape=jax.ShapeDtypeStruct((rows, ncol), BF16),
        scratch_shapes=[pltpu.VMEM((rows, ncol), F32)],
        compiler_params=pltpu.CompilerParams(vmem_limit_bytes=32 << 20),
        name="finish",
    )(parts, jnp.asarray(turn), row_code, col_code)


def iota(shape, axis):
    return lax.broadcasted_iota(jnp.int32, shape, axis)


def make_shards(ny, nx, nc):
    nzh, nzl = nx * nc * 2, 2
    swap = [(s, 1 - s) for s in range(2)]
    cross = [(s, 3 - s) for s in range(4)]

    def shards(amplitudes, integrals, occ_irrep, virt_irrep, slab_i, slab_j):
        vir, cblock = amplitudes.shape[1], amplitudes.shape[2]
        nk, q = integrals.shape[0], integrals.shape[2]
        ni = nzh * nzl
        na = vir // (ni * ny)
        zh, zl, y = lax.axis_index("zh"), lax.axis_index("zl"), lax.axis_index("y")
        x, c = lax.axis_index("x"), lax.axis_index("c")

        depth = -(-nk * cblock // LANES) * LANES
        w = integrals.transpose(2, 0, 1).reshape(q, nk * cblock)
        w = jnp.pad(w, ((0, 0), (0, depth - nk * cblock)))
        slot = zh // (2 * nc) * 2 + zh % 2
        last = jnp.where(iota((SENT - HALF, 1), 0) == slot, w[HALF:], 0)
        w = jnp.concatenate([w[:HALF], last], axis=0)

        t = amplitudes.reshape(vir // na, na * cblock)
        t = lax.all_to_all(t, ("zh", "zl"), 0, 0, tiled=True)
        w = lax.all_gather(w, "zh", axis=0, tiled=True)
        t, w = lax.optimization_barrier((t, w))
        w = w.reshape(nx, nc, 2, SENT, depth)
        kept = lax.dynamic_index_in_dim(w, c, 1, keepdims=False)
        given = lax.dynamic_index_in_dim(w, 1 - c, 1, keepdims=False)
        blocks = [kept, lax.ppermute(given, "c", swap), lax.ppermute(kept, "zl", swap), lax.ppermute(given, ("zl", "c"), cross)]
        t = lax.all_gather(t, "y", axis=0, tiled=True)
        t, blocks = lax.optimization_barrier((t, blocks))
        t_own = order_rows(t, nk, ny, ni, na, cblock, depth)
        t_other = lax.ppermute(t_own, "c", swap)

        parts = multiply(zl.reshape(1), t_own, t_other, blocks)
        tall = parts.shape[2]
        parts = lax.all_to_all(parts.reshape(ny * nx * tall, LANES), ("y", "x"), 0, 0, tiled=True)
        parts = parts.reshape(ny, nx, tall, LANES)

        a_index = ((zh * nzl + zl) * ny + y) * na + jnp.arange(na, dtype=jnp.int32)
        irr_virt_rows = lookup(virt_irrep, a_index)
        irr_occ_rows = lookup(occ_irrep, slab_i)
        row_code = jnp.bitwise_xor(irr_virt_rows[:, None], irr_occ_rows[None, :]).reshape(na * ni, 1)
        ncol = 2 * nzl * ny * q
        col_index = (x * nc + c) * ncol + jnp.arange(ncol, dtype=jnp.int32)
        irr_occ_cols = lookup(lookup(occ_irrep, slab_j), col_index // vir)
        irr_virt_cols = lookup(virt_irrep, col_index % vir)
        col_code = jnp.bitwise_xor(irr_occ_cols, irr_virt_cols)[None, :]
        out = finish(parts, row_code, col_code, q)
        return out.reshape(na, ni, ncol).transpose(1, 0, 2)

    return shards


def solution(mesh):
    nx, nc, ny = 4, 2, 4
    fine = Mesh(mesh.devices.reshape(nx * nc * 2, 2, ny, nx, nc), ("zh", "zl", "y", "x", "c"))
    row, rep = ("zh", "zl", "y"), ("x", "c")
    return jax.shard_map(
        make_shards(ny, nx, nc),
        mesh=fine,
        in_specs=(P(row, None, rep), P(None, rep, row), P(), P(), P(), P()),
        out_specs=P(None, row, rep),
        check_vma=False,
    )
```

```python
import jax
import jax.numpy as jnp
import numpy as np
from jax import lax
from jax.experimental import pallas as pl
from jax.experimental.pallas import tpu as pltpu
from jax.sharding import Mesh, PartitionSpec as P

BF16 = jnp.bfloat16
F32 = jnp.float32
LANES = 128
HALF = 64
SENT = 72
EXTRA = 16


def lookup(table, index):
    compare = index[:, None] == jnp.arange(table.shape[0], dtype=jnp.int32)[None, :]
    return jnp.sum(jnp.where(compare, table[None, :], 0), axis=1)


def dot(a, b, contract):
    return lax.dot_general(a, b, ((contract[:1], contract[1:]), ((), ())), preferred_element_type=F32)


def onehot(hit):
    return np.asarray(hit).astype(np.dtype(jnp.bfloat16))


def order_rows(gathered, nk, pieces, ni, na, cblock, depth):
    rows = ni * pieces
    to, at = np.indices((rows, rows))
    shuffle = onehot(at == to % ni * pieces + to // ni)
    at, to = np.indices((na * cblock, na * LANES))
    spread = onehot((at // cblock == to // LANES) & (at % cblock == to % LANES))
    at, to = np.indices((nk * LANES, depth))
    pack = onehot((at % LANES < cblock) & (to == at // LANES * cblock + at % LANES))

    def kernel(g_ref, s_ref, t_ref, u_ref, o_ref):
        wide = []
        for k in range(nk):
            rowed = dot(s_ref[...], g_ref[k * rows : (k + 1) * rows, :], (1, 0)).astype(BF16)
            wide.append(dot(rowed, t_ref[...], (1, 0)).astype(BF16))
        for a in range(na):
            at = slice(a * LANES, (a + 1) * LANES)
            block = dot(jnp.concatenate([part[:, at] for part in wide], axis=1), u_ref[...], (1, 0))
            o_ref[:, a * ni : (a + 1) * ni, :] = block.astype(BF16).reshape(pieces, ni, depth)

    return pl.pallas_call(
        kernel,
        out_shape=jax.ShapeDtypeStruct((pieces, na * ni, depth), BF16),
        compiler_params=pltpu.CompilerParams(vmem_limit_bytes=32 << 20),
        name="order_rows",
    )(gathered, jnp.asarray(shuffle), jnp.asarray(spread), jnp.asarray(pack))


def multiply(zl, a_own, a_other, blocks):
    pieces, rows, depth = a_own.shape
    nx, halves, tall, _ = blocks[0].shape
    step = min(2, pieces)
    to, at = np.indices((nx * EXTRA, 4 * (tall - HALF)))
    x, part, parity, half = to // EXTRA, to % EXTRA // 4, to % 4 // 2, to % 2
    pick = onehot((to % EXTRA < 8) & (at == (part * 2 + parity) * (tall - HALF) + x * halves + half))

    def kernel(zl_ref, a0_ref, a1_ref, b0, b1, b2, b3, pick_ref, o_ref, cols):
        @pl.when(pl.program_id(0) == 0)
        def _():
            for n, b_ref in enumerate((b0, b1, b2, b3)):
                parity = zl_ref[0] if n < 2 else 1 - zl_ref[0]
                spot = slice(n % 2 * depth, (n % 2 + 1) * depth)
                total = jnp.zeros((tall - HALF, depth), F32)
                for x in range(nx):
                    block = jnp.concatenate([b_ref[x, half, :HALF, :] for half in range(halves)], axis=0)
                    lane = pl.multiple_of((x * 2 + parity) * LANES, LANES)
                    cols[spot, pl.ds(lane, LANES)] = block.T
                    for half in range(halves):
                        total = total + b_ref[x, half, HALF:, :].astype(F32)
                total = jnp.concatenate([total, jnp.zeros((LANES - total.shape[0], depth), F32)], axis=0)
                lane = pl.multiple_of((nx * 2 + parity) * LANES, LANES)
                cols[spot, pl.ds(lane, LANES)] = total.astype(BF16).T

        a = jnp.concatenate([a0_ref[...].reshape(step * rows, depth), a1_ref[...].reshape(step * rows, depth)], axis=1)
        out = dot(a, cols[...], (1, 0))
        for p in range(step):
            own = out[p * rows : (p + 1) * rows]
            left = [own[:, at * LANES : (at + 1) * LANES].T[: tall - HALF] for at in (nx * 2, nx * 2 + 1)]
            blank = jnp.zeros((tall - HALF, 2 * LANES - rows), F32)
            left = [part[:, :LANES] for part in left] + [jnp.concatenate([part[:, LANES:], blank], axis=1) for part in left]
            left = dot(pick_ref[...], jnp.concatenate(left, axis=0).astype(BF16), (1, 0)).astype(BF16)
            for x in range(nx):
                for parity in range(2):
                    at = (x * 2 + parity) * LANES
                    o_ref[p, x, parity * rows : (parity + 1) * rows, :] = own[:, at : at + LANES].astype(BF16)
                o_ref[p, x, 2 * rows :, :] = left[x * EXTRA : (x + 1) * EXTRA]

    a_spec = pl.BlockSpec((step, rows, depth), lambda p, zl: (p, 0, 0))
    b_spec = pl.BlockSpec(blocks[0].shape, lambda p, zl: (0, 0, 0, 0))
    return pl.pallas_call(
        kernel,
        grid_spec=pltpu.PrefetchScalarGridSpec(
            num_scalar_prefetch=1,
            grid=(pieces // step,),
            in_specs=[a_spec, a_spec] + [b_spec] * 4 + [pl.BlockSpec(pick.shape, lambda p, zl: (0, 0))],
            out_specs=pl.BlockSpec((step, nx, 2 * rows + EXTRA, LANES), lambda p, zl: (p, 0, 0, 0)),
            scratch_shapes=[pltpu.VMEM((2 * depth, (nx + 1) * 2 * LANES), BF16)],
        ),
        out_shape=jax.ShapeDtypeStruct((pieces, nx, 2 * rows + EXTRA, LANES), BF16),
        compiler_params=pltpu.CompilerParams(vmem_limit_bytes=32 << 20),
        name="multiply",
    )(zl, a_own, a_other, *blocks, jnp.asarray(pick))


def finish(parts, row_code, col_code, q):
    pieces, nx, tall, _ = parts.shape
    rows = (tall - EXTRA) // 2
    ncol = col_code.shape[1]
    at, to = np.indices((EXTRA, 8))
    turn = onehot(at == to)

    def kernel(p_ref, turn_ref, r_ref, c_ref, o_ref, line):
        for p in range(pieces):
            total = p_ref[p, 0].astype(F32)
            for x in range(1, nx):
                total = total + p_ref[p, x].astype(F32)
            last = dot(total[2 * rows :].astype(BF16), turn_ref[...], (0, 0))
            for parity in range(2):
                for half in range(2):
                    at = ((half * 2 + parity) * pieces + p) * q
                    own = slice(parity * rows, (parity + 1) * rows)
                    line[:, at : at + HALF] = total[own, half * HALF : (half + 1) * HALF]
                    col = parity * 2 + half
                    line[:LANES, at + HALF : at + q] = last[:, col : col + 1]
                    line[LANES:, at + HALF : at + q] = last[: rows - LANES, 4 + col : 5 + col]
        kept = r_ref[...] == c_ref[...]
        o_ref[...] = jnp.where(kept, line[...], 0.0).astype(BF16)

    return pl.pallas_call(
        kernel,
        out_shape=jax.ShapeDtypeStruct((rows, ncol), BF16),
        scratch_shapes=[pltpu.VMEM((rows, ncol), F32)],
        compiler_params=pltpu.CompilerParams(vmem_limit_bytes=32 << 20),
        name="finish",
    )(parts, jnp.asarray(turn), row_code, col_code)


def iota(shape, axis):
    return lax.broadcasted_iota(jnp.int32, shape, axis)


def make_shards(ny, nx, nc):
    nzh, nzl = nx * nc * 2, 2
    swap = [(s, 1 - s) for s in range(2)]
    cross = [(s, 3 - s) for s in range(4)]

    def shards(amplitudes, integrals, occ_irrep, virt_irrep, slab_i, slab_j):
        vir, cblock = amplitudes.shape[1], amplitudes.shape[2]
        nk, q = integrals.shape[0], integrals.shape[2]
        ni = nzh * nzl
        na = vir // (ni * ny)
        zh, zl, y = lax.axis_index("zh"), lax.axis_index("zl"), lax.axis_index("y")
        x, c = lax.axis_index("x"), lax.axis_index("c")

        depth = -(-nk * cblock // LANES) * LANES
        w = integrals.transpose(2, 0, 1).reshape(q, nk * cblock)
        w = jnp.pad(w, ((0, 0), (0, depth - nk * cblock)))
        slot = zh // (2 * nc) * 2 + zh % 2
        last = jnp.where(iota((SENT - HALF, 1), 0) == slot, w[HALF:], 0)
        w = jnp.concatenate([w[:HALF], last], axis=0)

        t = amplitudes.reshape(vir // na, na * cblock)
        w = lax.all_gather(w, "zh", axis=0, tiled=True)
        t, w = lax.optimization_barrier((t, w))
        t = lax.all_to_all(t, ("zh", "zl"), 0, 0, tiled=True)
        w = w.reshape(nx, nc, 2, SENT, depth)
        kept = lax.dynamic_index_in_dim(w, c, 1, keepdims=False)
        given = lax.dynamic_index_in_dim(w, 1 - c, 1, keepdims=False)
        blocks = [kept, lax.ppermute(given, "c", swap), lax.ppermute(kept, "zl", swap), lax.ppermute(given, ("zl", "c"), cross)]
        t = lax.all_gather(t, "y", axis=0, tiled=True)
        t, blocks = lax.optimization_barrier((t, blocks))
        t_own = order_rows(t, nk, ny, ni, na, cblock, depth)
        t_other = lax.ppermute(t_own, "c", swap)

        parts = multiply(zl.reshape(1), t_own, t_other, blocks)
        tall = parts.shape[2]
        parts = lax.all_to_all(parts.reshape(ny * nx * tall, LANES), ("y", "x"), 0, 0, tiled=True)
        parts = parts.reshape(ny, nx, tall, LANES)

        a_index = ((zh * nzl + zl) * ny + y) * na + jnp.arange(na, dtype=jnp.int32)
        irr_virt_rows = lookup(virt_irrep, a_index)
        irr_occ_rows = lookup(occ_irrep, slab_i)
        row_code = jnp.bitwise_xor(irr_virt_rows[:, None], irr_occ_rows[None, :]).reshape(na * ni, 1)
        ncol = 2 * nzl * ny * q
        col_index = (x * nc + c) * ncol + jnp.arange(ncol, dtype=jnp.int32)
        irr_occ_cols = lookup(lookup(occ_irrep, slab_j), col_index // vir)
        irr_virt_cols = lookup(virt_irrep, col_index % vir)
        col_code = jnp.bitwise_xor(irr_occ_cols, irr_virt_cols)[None, :]
        out = finish(parts, row_code, col_code, q)
        return out.reshape(na, ni, ncol).transpose(1, 0, 2)

    return shards


def solution(mesh):
    nx, nc, ny = 4, 2, 4
    fine = Mesh(mesh.devices.reshape(nx * nc * 2, 2, ny, nx, nc), ("zh", "zl", "y", "x", "c"))
    row, rep = ("zh", "zl", "y"), ("x", "c")
    return jax.shard_map(
        make_shards(ny, nx, nc),
        mesh=fine,
        in_specs=(P(row, None, rep), P(None, rep, row), P(), P(), P(), P()),
        out_specs=P(None, row, rep),
        check_vma=False,
    )
```

```python
import jax
import jax.numpy as jnp
import numpy as np
from jax import lax
from jax.experimental import pallas as pl
from jax.experimental.pallas import tpu as pltpu
from jax.sharding import Mesh, PartitionSpec as P

BF16 = jnp.bfloat16
F32 = jnp.float32
LANES = 128
HALF = 64
SENT = 176
EXTRA = 16


def lookup(table, index):
    compare = index[:, None] == jnp.arange(table.shape[0], dtype=jnp.int32)[None, :]
    return jnp.sum(jnp.where(compare, table[None, :], 0), axis=1)


def dot(a, b, contract):
    return lax.dot_general(a, b, ((contract[:1], contract[1:]), ((), ())), preferred_element_type=F32)


def onehot(hit):
    return np.asarray(hit).astype(np.dtype(jnp.bfloat16))


def order_rows(gathered, nk, pieces, ni, na, cblock, depth):
    rows = ni * pieces
    to, at = np.indices((rows, rows))
    shuffle = onehot(at == to % ni * pieces + to // ni)
    at, to = np.indices((na * cblock, na * LANES))
    spread = onehot((at // cblock == to // LANES) & (at % cblock == to % LANES))
    at, to = np.indices((nk * LANES, depth))
    pack = onehot((at % LANES < cblock) & (to == at // LANES * cblock + at % LANES))

    def kernel(g_ref, s_ref, t_ref, u_ref, o_ref):
        wide = []
        for k in range(nk):
            rowed = dot(s_ref[...], g_ref[k * rows : (k + 1) * rows, :], (1, 0)).astype(BF16)
            wide.append(dot(rowed, t_ref[...], (1, 0)).astype(BF16))
        for a in range(na):
            at = slice(a * LANES, (a + 1) * LANES)
            block = dot(jnp.concatenate([part[:, at] for part in wide], axis=1), u_ref[...], (1, 0))
            o_ref[:, a * ni : (a + 1) * ni, :] = block.astype(BF16).reshape(pieces, ni, depth)

    return pl.pallas_call(
        kernel,
        out_shape=jax.ShapeDtypeStruct((pieces, na * ni, depth), BF16),
        compiler_params=pltpu.CompilerParams(vmem_limit_bytes=32 << 20),
        name="order_rows",
    )(gathered, jnp.asarray(shuffle), jnp.asarray(spread), jnp.asarray(pack))


def pack_columns(w):
    fold = HALF // 2

    def kernel(w_ref, o_ref):
        w = w_ref[...].astype(F32)
        third = w[:HALF, 2 * LANES :]
        third = jnp.concatenate([third[:fold], third[fold:]], axis=1)
        end = w[HALF:, 2 * LANES :]
        last = [w[HALF:, :LANES], w[HALF:, LANES : 2 * LANES], jnp.concatenate([end, jnp.zeros_like(end)], axis=1)]
        last += [jnp.zeros((EXTRA - 3, LANES), F32)]
        packed = [w[:HALF, :LANES], w[:HALF, LANES : 2 * LANES], third, jnp.concatenate(last, axis=0)]
        o_ref[...] = jnp.concatenate(packed, axis=0).astype(BF16)

    return pl.pallas_call(
        kernel,
        out_shape=jax.ShapeDtypeStruct((SENT, LANES), BF16),
        compiler_params=pltpu.CompilerParams(vmem_limit_bytes=32 << 20),
        name="pack_columns",
    )(w)


def multiply(zl, a_own, a_other, blocks):
    pieces, rows, depth = a_own.shape
    nx, halves = blocks[0].shape[:2]
    slots = nx * halves
    step = min(2, pieces)
    fold = HALF // 2
    at, to = np.indices((slots * EXTRA, 3 * LANES))
    turn = onehot((at % EXTRA == to // LANES) & (at // EXTRA == to % LANES))
    to, at = np.indices((nx * EXTRA, 4 * slots))
    x, part, parity, half = to // EXTRA, to % EXTRA // 4, to % 4 // 2, to % 2
    pick = onehot((to % EXTRA < 8) & (at == (part * 2 + parity) * slots + x * halves + half))

    def kernel(zl_ref, a0_ref, a1_ref, b0, b1, b2, b3, turn_ref, pick_ref, o_ref, cols):
        @pl.when(pl.program_id(0) == 0)
        def _():
            for n, b_ref in enumerate((b0, b1, b2, b3)):
                parity = zl_ref[0] if n < 2 else 1 - zl_ref[0]
                first = n % 2 * depth
                for x in range(nx):
                    lane = pl.ds(pl.multiple_of((x * 2 + parity) * LANES, LANES), LANES)
                    for tile in range(2):
                        rows_of = [slice(at, at + fold) for at in (tile * HALF, tile * HALF + fold)]
                        block = jnp.concatenate([b_ref[x, half, at, :] for at in rows_of for half in range(halves)], axis=0)
                        cols[first + tile * LANES : first + (tile + 1) * LANES, lane] = block.T
                    block = jnp.concatenate([b_ref[x, half, 2 * HALF : 2 * HALF + fold, :] for half in range(halves)], axis=0)
                    block = block.astype(F32).T
                    block = jnp.concatenate([block[:HALF], block[HALF:]], axis=1)
                    block = jnp.concatenate([block, jnp.zeros_like(block)], axis=0)
                    cols[first + 2 * LANES : first + 3 * LANES, lane] = block.astype(BF16)
                lane = pl.ds(pl.multiple_of((nx * 2 + parity) * LANES, LANES), LANES)
                last = jnp.concatenate([b_ref[x, half, SENT - EXTRA :, :] for x in range(nx) for half in range(halves)], axis=0)
                last = dot(last, turn_ref[...], (0, 0)).astype(BF16)
                for tile in range(3):
                    cols[first + tile * LANES : first + (tile + 1) * LANES, lane] = last[:, tile * LANES : (tile + 1) * LANES]

        a = jnp.concatenate([a0_ref[...].reshape(step * rows, depth), a1_ref[...].reshape(step * rows, depth)], axis=1)
        out = dot(a, cols[...], (1, 0))
        for p in range(step):
            own = out[p * rows : (p + 1) * rows]
            left = [own[:, at * LANES : (at + 1) * LANES].T[:slots] for at in (nx * 2, nx * 2 + 1)]
            blank = jnp.zeros((slots, 2 * LANES - rows), F32)
            left = [part[:, :LANES] for part in left] + [jnp.concatenate([part[:, LANES:], blank], axis=1) for part in left]
            left = dot(pick_ref[...], jnp.concatenate(left, axis=0).astype(BF16), (1, 0)).astype(BF16)
            for x in range(nx):
                for parity in range(2):
                    at = (x * 2 + parity) * LANES
                    o_ref[p, x, parity * rows : (parity + 1) * rows, :] = own[:, at : at + LANES].astype(BF16)
                o_ref[p, x, 2 * rows :, :] = left[x * EXTRA : (x + 1) * EXTRA]

    a_spec = pl.BlockSpec((step, rows, depth), lambda p, zl: (p, 0, 0))
    b_spec = pl.BlockSpec(blocks[0].shape, lambda p, zl: (0, 0, 0, 0))
    return pl.pallas_call(
        kernel,
        grid_spec=pltpu.PrefetchScalarGridSpec(
            num_scalar_prefetch=1,
            grid=(pieces // step,),
            in_specs=[a_spec, a_spec] + [b_spec] * 4 + [pl.BlockSpec(m.shape, lambda p, zl: (0, 0)) for m in (turn, pick)],
            out_specs=pl.BlockSpec((step, nx, 2 * rows + EXTRA, LANES), lambda p, zl: (p, 0, 0, 0)),
            scratch_shapes=[pltpu.VMEM((2 * depth, (nx + 1) * 2 * LANES), BF16)],
        ),
        out_shape=jax.ShapeDtypeStruct((pieces, nx, 2 * rows + EXTRA, LANES), BF16),
        compiler_params=pltpu.CompilerParams(vmem_limit_bytes=32 << 20),
        name="multiply",
    )(zl, a_own, a_other, *blocks, jnp.asarray(turn), jnp.asarray(pick))


def finish(parts, row_code, col_code, q):
    pieces, nx, tall, _ = parts.shape
    rows = (tall - EXTRA) // 2
    ncol = col_code.shape[1]
    fold = HALF // 2
    at, to = np.indices((EXTRA, 8))
    turn = onehot(at == to)

    def kernel(p_ref, turn_ref, r_ref, c_ref, o_ref, line):
        for p in range(pieces):
            total = p_ref[p, 0].astype(F32)
            for x in range(1, nx):
                total = total + p_ref[p, x].astype(F32)
            last = dot(total[2 * rows :].astype(BF16), turn_ref[...], (0, 0))
            for parity in range(2):
                for half in range(2):
                    at = ((half * 2 + parity) * pieces + p) * q
                    own = slice(parity * rows, (parity + 1) * rows)
                    for part in range(2):
                        lane = part * HALF + half * fold
                        line[:, at + part * fold : at + (part + 1) * fold] = total[own, lane : lane + fold]
                    col = parity * 2 + half
                    line[:LANES, at + HALF : at + q] = last[:, col : col + 1]
                    line[LANES:, at + HALF : at + q] = last[: rows - LANES, 4 + col : 5 + col]
        kept = r_ref[...] == c_ref[...]
        o_ref[...] = jnp.where(kept, line[...], 0.0).astype(BF16)

    return pl.pallas_call(
        kernel,
        out_shape=jax.ShapeDtypeStruct((rows, ncol), BF16),
        scratch_shapes=[pltpu.VMEM((rows, ncol), F32)],
        compiler_params=pltpu.CompilerParams(vmem_limit_bytes=32 << 20),
        name="finish",
    )(parts, jnp.asarray(turn), row_code, col_code)


def make_shards(ny, nx, nc):
    nzh, nzl = nx * nc * 2, 2
    swap = [(s, 1 - s) for s in range(2)]
    cross = [(s, 3 - s) for s in range(4)]

    def shards(amplitudes, integrals, occ_irrep, virt_irrep, slab_i, slab_j):
        vir, cblock = amplitudes.shape[1], amplitudes.shape[2]
        nk, q = integrals.shape[0], integrals.shape[2]
        ni = nzh * nzl
        na = vir // (ni * ny)
        zh, zl, y = lax.axis_index("zh"), lax.axis_index("zl"), lax.axis_index("y")
        x, c = lax.axis_index("x"), lax.axis_index("c")

        depth = -(-nk * cblock // LANES) * LANES
        w = pack_columns(integrals.transpose(2, 0, 1).reshape(q, nk * cblock))

        t = amplitudes.reshape(vir // na, na * cblock)
        w = lax.all_gather(w, "zh", axis=0, tiled=True)
        t, w = lax.optimization_barrier((t, w))
        t = lax.all_to_all(t, ("zh", "zl"), 0, 0, tiled=True)
        w = w.reshape(nx, nc, 2, SENT, LANES)
        kept = lax.dynamic_index_in_dim(w, c, 1, keepdims=False)
        given = lax.dynamic_index_in_dim(w, 1 - c, 1, keepdims=False)
        blocks = [kept, lax.ppermute(given, "c", swap), lax.ppermute(kept, "zl", swap), lax.ppermute(given, ("zl", "c"), cross)]
        t = lax.all_gather(t, "y", axis=0, tiled=True)
        t, blocks = lax.optimization_barrier((t, blocks))
        t_own = order_rows(t, nk, ny, ni, na, cblock, depth)
        t_other = lax.ppermute(t_own, "c", swap)

        parts = multiply(zl.reshape(1), t_own, t_other, blocks)
        tall = parts.shape[2]
        parts = lax.all_to_all(parts.reshape(ny * nx * tall, LANES), ("y", "x"), 0, 0, tiled=True)
        parts = parts.reshape(ny, nx, tall, LANES)

        a_index = ((zh * nzl + zl) * ny + y) * na + jnp.arange(na, dtype=jnp.int32)
        irr_virt_rows = lookup(virt_irrep, a_index)
        irr_occ_rows = lookup(occ_irrep, slab_i)
        row_code = jnp.bitwise_xor(irr_virt_rows[:, None], irr_occ_rows[None, :]).reshape(na * ni, 1)
        ncol = 2 * nzl * ny * q
        col_index = (x * nc + c) * ncol + jnp.arange(ncol, dtype=jnp.int32)
        irr_occ_cols = lookup(lookup(occ_irrep, slab_j), col_index // vir)
        irr_virt_cols = lookup(virt_irrep, col_index % vir)
        col_code = jnp.bitwise_xor(irr_occ_cols, irr_virt_cols)[None, :]
        out = finish(parts, row_code, col_code, q)
        return out.reshape(na, ni, ncol).transpose(1, 0, 2)

    return shards


def solution(mesh):
    nx, nc, ny = 4, 2, 4
    fine = Mesh(mesh.devices.reshape(nx * nc * 2, 2, ny, nx, nc), ("zh", "zl", "y", "x", "c"))
    row, rep = ("zh", "zl", "y"), ("x", "c")
    return jax.shard_map(
        make_shards(ny, nx, nc),
        mesh=fine,
        in_specs=(P(row, None, rep), P(None, rep, row), P(), P(), P(), P()),
        out_specs=P(None, row, rep),
        check_vma=False,
    )
```

```python
import jax
import jax.numpy as jnp
import numpy as np
from jax import lax
from jax.experimental import pallas as pl
from jax.experimental.pallas import tpu as pltpu
from jax.sharding import Mesh, PartitionSpec as P

BF16 = jnp.bfloat16
F32 = jnp.float32
LANES = 128
HALF = 64
SENT = 176
EXTRA = 16


def lookup(table, index):
    compare = index[:, None] == jnp.arange(table.shape[0], dtype=jnp.int32)[None, :]
    return jnp.sum(jnp.where(compare, table[None, :], 0), axis=1)


def dot(a, b, contract):
    return lax.dot_general(a, b, ((contract[:1], contract[1:]), ((), ())), preferred_element_type=F32)


def onehot(hit):
    return np.asarray(hit).astype(np.dtype(jnp.bfloat16))


def order_rows(gathered, nk, pieces, ni, na, cblock, depth):
    rows = ni * pieces
    to, at = np.indices((rows, rows))
    shuffle = onehot(at == to % ni * pieces + to // ni)
    at, to = np.indices((na * cblock, na * LANES))
    spread = onehot((at // cblock == to // LANES) & (at % cblock == to % LANES))
    at, to = np.indices((nk * LANES, depth))
    pack = onehot((at % LANES < cblock) & (to == at // LANES * cblock + at % LANES))

    def kernel(g_ref, s_ref, t_ref, u_ref, o_ref):
        wide = []
        for k in range(nk):
            rowed = dot(s_ref[...], g_ref[k * rows : (k + 1) * rows, :], (1, 0)).astype(BF16)
            wide.append(dot(rowed, t_ref[...], (1, 0)).astype(BF16))
        for a in range(na):
            at = slice(a * LANES, (a + 1) * LANES)
            block = dot(jnp.concatenate([part[:, at] for part in wide], axis=1), u_ref[...], (1, 0))
            o_ref[:, a * ni : (a + 1) * ni, :] = block.astype(BF16).reshape(pieces, ni, depth)

    return pl.pallas_call(
        kernel,
        out_shape=jax.ShapeDtypeStruct((pieces, na * ni, depth), BF16),
        compiler_params=pltpu.CompilerParams(vmem_limit_bytes=32 << 20),
        name="order_rows",
    )(gathered, jnp.asarray(shuffle), jnp.asarray(spread), jnp.asarray(pack))


def pack_columns(w):
    fold = HALF // 2

    def kernel(w_ref, o_ref):
        w = w_ref[...].astype(F32)
        third = w[:HALF, 2 * LANES :]
        third = jnp.concatenate([third[:fold], third[fold:]], axis=1)
        end = w[HALF:, 2 * LANES :]
        last = [w[HALF:, :LANES], w[HALF:, LANES : 2 * LANES], jnp.concatenate([end, jnp.zeros_like(end)], axis=1)]
        last += [jnp.zeros((EXTRA - 3, LANES), F32)]
        packed = [w[:HALF, :LANES], w[:HALF, LANES : 2 * LANES], third, jnp.concatenate(last, axis=0)]
        o_ref[...] = jnp.concatenate(packed, axis=0).astype(BF16)

    return pl.pallas_call(
        kernel,
        out_shape=jax.ShapeDtypeStruct((SENT, LANES), BF16),
        compiler_params=pltpu.CompilerParams(vmem_limit_bytes=32 << 20),
        name="pack_columns",
    )(w)


def multiply(zl, a_own, a_other, blocks):
    pieces, rows, depth = a_own.shape
    nx, halves = blocks[0].shape[:2]
    slots = nx * halves
    step = min(2, pieces)
    fold = HALF // 2
    at, to = np.indices((slots * EXTRA, 3 * LANES))
    turn = onehot((at % EXTRA == to // LANES) & (at // EXTRA == to % LANES))
    to, at = np.indices((nx * EXTRA, 4 * slots))
    x, part, parity, half = to // EXTRA, to % EXTRA // 4, to % 4 // 2, to % 2
    pick = onehot((to % EXTRA < 8) & (at == (part * 2 + parity) * slots + x * halves + half))

    def kernel(zl_ref, a0_ref, a1_ref, b0, b1, b2, b3, turn_ref, pick_ref, o_ref, cols):
        @pl.when(pl.program_id(0) == 0)
        def _():
            for n, b_ref in enumerate((b0, b1, b2, b3)):
                parity = zl_ref[0] if n < 2 else 1 - zl_ref[0]
                first = n % 2 * depth
                for x in range(nx):
                    lane = pl.ds(pl.multiple_of((x * 2 + parity) * LANES, LANES), LANES)
                    for tile in range(2):
                        rows_of = [slice(at, at + fold) for at in (tile * HALF, tile * HALF + fold)]
                        block = jnp.concatenate([b_ref[x, half, at, :] for at in rows_of for half in range(halves)], axis=0)
                        cols[first + tile * LANES : first + (tile + 1) * LANES, lane] = block.T
                    block = jnp.concatenate([b_ref[x, half, 2 * HALF : 2 * HALF + fold, :] for half in range(halves)], axis=0)
                    block = block.astype(F32).T
                    block = jnp.concatenate([block[:HALF], block[HALF:]], axis=1)
                    block = jnp.concatenate([block, jnp.zeros_like(block)], axis=0)
                    cols[first + 2 * LANES : first + 3 * LANES, lane] = block.astype(BF16)
                lane = pl.ds(pl.multiple_of((nx * 2 + parity) * LANES, LANES), LANES)
                last = jnp.concatenate([b_ref[x, half, SENT - EXTRA :, :] for x in range(nx) for half in range(halves)], axis=0)
                last = dot(last, turn_ref[...], (0, 0)).astype(BF16)
                for tile in range(3):
                    cols[first + tile * LANES : first + (tile + 1) * LANES, lane] = last[:, tile * LANES : (tile + 1) * LANES]

        a = jnp.concatenate([a0_ref[...].reshape(step * rows, depth), a1_ref[...].reshape(step * rows, depth)], axis=1)
        out = dot(a, cols[...], (1, 0))
        for p in range(step):
            own = out[p * rows : (p + 1) * rows]
            left = [own[:, at * LANES : (at + 1) * LANES].T[:slots] for at in (nx * 2, nx * 2 + 1)]
            blank = jnp.zeros((slots, 2 * LANES - rows), F32)
            left = [part[:, :LANES] for part in left] + [jnp.concatenate([part[:, LANES:], blank], axis=1) for part in left]
            left = dot(pick_ref[...], jnp.concatenate(left, axis=0).astype(BF16), (1, 0)).astype(BF16)
            for x in range(nx):
                for parity in range(2):
                    at = (x * 2 + parity) * LANES
                    o_ref[p, x, parity * rows : (parity + 1) * rows, :] = own[:, at : at + LANES].astype(BF16)
                o_ref[p, x, 2 * rows :, :] = left[x * EXTRA : (x + 1) * EXTRA]

    a_spec = pl.BlockSpec((step, rows, depth), lambda p, zl: (p, 0, 0))
    b_spec = pl.BlockSpec(blocks[0].shape, lambda p, zl: (0, 0, 0, 0))
    return pl.pallas_call(
        kernel,
        grid_spec=pltpu.PrefetchScalarGridSpec(
            num_scalar_prefetch=1,
            grid=(pieces // step,),
            in_specs=[a_spec, a_spec] + [b_spec] * 4 + [pl.BlockSpec(m.shape, lambda p, zl: (0, 0)) for m in (turn, pick)],
            out_specs=pl.BlockSpec((step, nx, 2 * rows + EXTRA, LANES), lambda p, zl: (p, 0, 0, 0)),
            scratch_shapes=[pltpu.VMEM((2 * depth, (nx + 1) * 2 * LANES), BF16)],
        ),
        out_shape=jax.ShapeDtypeStruct((pieces, nx, 2 * rows + EXTRA, LANES), BF16),
        compiler_params=pltpu.CompilerParams(vmem_limit_bytes=32 << 20),
        name="multiply",
    )(zl, a_own, a_other, *blocks, jnp.asarray(turn), jnp.asarray(pick))


def finish(parts, row_code, col_code, q):
    pieces, nx, tall, _ = parts.shape
    rows = (tall - EXTRA) // 2
    ncol = col_code.shape[1]
    fold = HALF // 2
    at, to = np.indices((EXTRA, 8))
    turn = onehot(at == to)

    def kernel(p_ref, turn_ref, r_ref, c_ref, o_ref, line):
        for p in range(pieces):
            total = p_ref[p, 0].astype(F32)
            for x in range(1, nx):
                total = total + p_ref[p, x].astype(F32)
            last = dot(total[2 * rows :].astype(BF16), turn_ref[...], (0, 0))
            for parity in range(2):
                for half in range(2):
                    at = ((half * 2 + parity) * pieces + p) * q
                    own = slice(parity * rows, (parity + 1) * rows)
                    for part in range(2):
                        lane = part * HALF + half * fold
                        line[:, at + part * fold : at + (part + 1) * fold] = total[own, lane : lane + fold]
                    col = parity * 2 + half
                    line[:LANES, at + HALF : at + q] = last[:, col : col + 1]
                    line[LANES:, at + HALF : at + q] = last[: rows - LANES, 4 + col : 5 + col]
        kept = r_ref[...] == c_ref[...]
        o_ref[...] = jnp.where(kept, line[...], 0.0).astype(BF16)

    return pl.pallas_call(
        kernel,
        out_shape=jax.ShapeDtypeStruct((rows, ncol), BF16),
        scratch_shapes=[pltpu.VMEM((rows, ncol), F32)],
        compiler_params=pltpu.CompilerParams(vmem_limit_bytes=32 << 20),
        name="finish",
    )(parts, jnp.asarray(turn), row_code, col_code)


def make_shards(ny, nx, nc):
    nzh, nzl = nx * nc * 2, 2
    swap = [(s, 1 - s) for s in range(2)]

    def shards(amplitudes, integrals, occ_irrep, virt_irrep, slab_i, slab_j):
        vir, cblock = amplitudes.shape[1], amplitudes.shape[2]
        nk, q = integrals.shape[0], integrals.shape[2]
        ni = nzh * nzl
        na = vir // (ni * ny)
        zh, zl, y = lax.axis_index("zh"), lax.axis_index("zl"), lax.axis_index("y")
        x, c = lax.axis_index("x"), lax.axis_index("c")

        depth = -(-nk * cblock // LANES) * LANES
        w = pack_columns(integrals.transpose(2, 0, 1).reshape(q, nk * cblock))

        t = amplitudes.reshape(vir // na, na * cblock)
        t = lax.all_to_all(t, ("zh", "zl"), 0, 0, tiled=True)
        t, w = lax.optimization_barrier((t, w))
        t = lax.all_to_all(jnp.broadcast_to(t, (ny, *t.shape)), "y", 0, 0)
        w = lax.all_gather(w, "zh", axis=0, tiled=True)
        t, w = lax.optimization_barrier((t.reshape(-1, na * cblock), w))
        w = w.reshape(nx, nc, 2, SENT, LANES)
        kept = lax.dynamic_index_in_dim(w, c, 1, keepdims=False)
        given = lax.dynamic_index_in_dim(w, 1 - c, 1, keepdims=False)
        up = [(s, (s + 1) % ni) for s in range(ni)]
        down = [(s * nc + core, (s - 1) % ni * nc + 1 - core) for s in range(ni) for core in range(nc)]
        blocks = [
            kept,
            lax.ppermute(given, "c", swap),
            lax.ppermute(kept, ("zh", "zl"), up),
            lax.ppermute(given, ("zh", "zl", "c"), down),
        ]
        t_own = order_rows(t, nk, ny, ni, na, cblock, depth)
        t_other = lax.ppermute(t_own, "c", swap)

        parts = multiply(zl.reshape(1), t_own, t_other, blocks)
        tall = parts.shape[2]
        parts = lax.all_to_all(parts.reshape(ny * nx * tall, LANES), ("y", "x"), 0, 0, tiled=True)
        parts = parts.reshape(ny, nx, tall, LANES)

        a_index = ((zh * nzl + zl) * ny + y) * na + jnp.arange(na, dtype=jnp.int32)
        irr_virt_rows = lookup(virt_irrep, a_index)
        irr_occ_rows = lookup(occ_irrep, slab_i)
        row_code = jnp.bitwise_xor(irr_virt_rows[:, None], irr_occ_rows[None, :]).reshape(na * ni, 1)
        ncol = 2 * nzl * ny * q
        col_index = (x * nc + c) * ncol + jnp.arange(ncol, dtype=jnp.int32)
        irr_occ_cols = lookup(lookup(occ_irrep, slab_j), col_index // vir)
        irr_virt_cols = lookup(virt_irrep, col_index % vir)
        col_code = jnp.bitwise_xor(irr_occ_cols, irr_virt_cols)[None, :]
        out = finish(parts, row_code, col_code, q)
        return out.reshape(na, ni, ncol).transpose(1, 0, 2)

    return shards


def solution(mesh):
    nx, nc, ny = 4, 2, 4
    fine = Mesh(mesh.devices.reshape(nx * nc * 2, 2, ny, nx, nc), ("zh", "zl", "y", "x", "c"))
    row, rep = ("zh", "zl", "y"), ("x", "c")
    return jax.shard_map(
        make_shards(ny, nx, nc),
        mesh=fine,
        in_specs=(P(row, None, rep), P(None, rep, row), P(), P(), P(), P()),
        out_specs=P(None, row, rep),
        check_vma=False,
    )
```

```python
import jax
import jax.numpy as jnp
import numpy as np
from jax import lax
from jax.experimental import pallas as pl
from jax.experimental.pallas import tpu as pltpu
from jax.sharding import Mesh, PartitionSpec as P

BF16 = jnp.bfloat16
F32 = jnp.float32
LANES = 128
HALF = 64
SENT = 176
EXTRA = 16


def lookup(table, index):
    compare = index[:, None] == jnp.arange(table.shape[0], dtype=jnp.int32)[None, :]
    return jnp.sum(jnp.where(compare, table[None, :], 0), axis=1)


def dot(a, b, contract):
    return lax.dot_general(a, b, ((contract[:1], contract[1:]), ((), ())), preferred_element_type=F32)


def onehot(hit):
    return np.asarray(hit).astype(np.dtype(jnp.bfloat16))


def order_rows(gathered, nk, nc, pieces, ni, na, cblock, depth):
    rows = ni * pieces
    to, at = np.indices((rows, rows))
    shuffle = onehot(at == to % ni * pieces + to // ni)
    at, to = np.indices((na * cblock, na * LANES))
    spread = onehot((at // cblock == to // LANES) & (at % cblock == to % LANES))
    at, to = np.indices((nk * LANES, depth))
    pack = onehot((at % LANES < cblock) & (to == at // LANES * cblock + at % LANES))

    def kernel(g_ref, s_ref, t_ref, u_ref, o_ref):
        for core in range(nc):
            wide = []
            for k in range(nk):
                first = (k * nc + core) * rows
                rowed = dot(s_ref[...], g_ref[first : first + rows, :], (1, 0)).astype(BF16)
                wide.append(dot(rowed, t_ref[...], (1, 0)).astype(BF16))
            for a in range(na):
                at = slice(a * LANES, (a + 1) * LANES)
                block = dot(jnp.concatenate([part[:, at] for part in wide], axis=1), u_ref[...], (1, 0))
                block = block.astype(BF16).reshape(pieces, ni, depth)
                o_ref[:, a * ni : (a + 1) * ni, core * depth : (core + 1) * depth] = block

    return pl.pallas_call(
        kernel,
        out_shape=jax.ShapeDtypeStruct((pieces, na * ni, nc * depth), BF16),
        compiler_params=pltpu.CompilerParams(vmem_limit_bytes=32 << 20),
        name="order_rows",
    )(gathered, jnp.asarray(shuffle), jnp.asarray(spread), jnp.asarray(pack))


def pack_columns(w):
    fold = HALF // 2

    def kernel(w_ref, o_ref):
        w = w_ref[...].astype(F32)
        third = w[:HALF, 2 * LANES :]
        third = jnp.concatenate([third[:fold], third[fold:]], axis=1)
        end = w[HALF:, 2 * LANES :]
        last = [w[HALF:, :LANES], w[HALF:, LANES : 2 * LANES], jnp.concatenate([end, jnp.zeros_like(end)], axis=1)]
        last += [jnp.zeros((EXTRA - 3, LANES), F32)]
        packed = [w[:HALF, :LANES], w[:HALF, LANES : 2 * LANES], third, jnp.concatenate(last, axis=0)]
        o_ref[...] = jnp.concatenate(packed, axis=0).astype(BF16)

    return pl.pallas_call(
        kernel,
        out_shape=jax.ShapeDtypeStruct((SENT, LANES), BF16),
        compiler_params=pltpu.CompilerParams(vmem_limit_bytes=32 << 20),
        name="pack_columns",
    )(w)


def multiply(zl, a, blocks):
    pieces, rows, deep = a.shape
    nx, halves, nc = blocks[0].shape[:3]
    depth = deep // nc
    slots = nx * halves
    step = min(2, pieces)
    fold = HALF // 2
    at, to = np.indices((slots * EXTRA, 3 * LANES))
    turn = onehot((at % EXTRA == to // LANES) & (at // EXTRA == to % LANES))
    to, at = np.indices((nx * EXTRA, 4 * slots))
    x, part, parity, half = to // EXTRA, to % EXTRA // 4, to % 4 // 2, to % 2
    pick = onehot((to % EXTRA < 8) & (at == (part * 2 + parity) * slots + x * halves + half))

    def kernel(zl_ref, a_ref, b0, b1, turn_ref, pick_ref, o_ref, cols):
        @pl.when(pl.program_id(0) == 0)
        def _():
            for n in range(2 * nc):
                b_ref, core = (b0, b1)[n // nc], n % nc
                parity = zl_ref[0] if n < nc else 1 - zl_ref[0]
                first = core * depth
                for x in range(nx):
                    lane = pl.ds(pl.multiple_of((x * 2 + parity) * LANES, LANES), LANES)
                    for tile in range(2):
                        rows_of = [slice(at, at + fold) for at in (tile * HALF, tile * HALF + fold)]
                        block = jnp.concatenate([b_ref[x, half, core, at, :] for at in rows_of for half in range(halves)], axis=0)
                        cols[first + tile * LANES : first + (tile + 1) * LANES, lane] = block.T
                    block = jnp.concatenate([b_ref[x, half, core, 2 * HALF : 2 * HALF + fold, :] for half in range(halves)], axis=0)
                    block = block.astype(F32).T
                    block = jnp.concatenate([block[:HALF], block[HALF:]], axis=1)
                    block = jnp.concatenate([block, jnp.zeros_like(block)], axis=0)
                    cols[first + 2 * LANES : first + 3 * LANES, lane] = block.astype(BF16)
                lane = pl.ds(pl.multiple_of((nx * 2 + parity) * LANES, LANES), LANES)
                last = jnp.concatenate([b_ref[x, half, core, SENT - EXTRA :, :] for x in range(nx) for half in range(halves)], axis=0)
                last = dot(last, turn_ref[...], (0, 0)).astype(BF16)
                for tile in range(3):
                    cols[first + tile * LANES : first + (tile + 1) * LANES, lane] = last[:, tile * LANES : (tile + 1) * LANES]

        out = dot(a_ref[...].reshape(step * rows, deep), cols[...], (1, 0))
        for p in range(step):
            own = out[p * rows : (p + 1) * rows]
            left = [own[:, at * LANES : (at + 1) * LANES].T[:slots] for at in (nx * 2, nx * 2 + 1)]
            blank = jnp.zeros((slots, 2 * LANES - rows), F32)
            left = [part[:, :LANES] for part in left] + [jnp.concatenate([part[:, LANES:], blank], axis=1) for part in left]
            left = dot(pick_ref[...], jnp.concatenate(left, axis=0).astype(BF16), (1, 0)).astype(BF16)
            for x in range(nx):
                for parity in range(2):
                    at = (x * 2 + parity) * LANES
                    o_ref[p, x, parity * rows : (parity + 1) * rows, :] = own[:, at : at + LANES].astype(BF16)
                o_ref[p, x, 2 * rows :, :] = left[x * EXTRA : (x + 1) * EXTRA]

    a_spec = pl.BlockSpec((step, rows, deep), lambda p, zl: (p, 0, 0))
    b_spec = pl.BlockSpec(blocks[0].shape, lambda p, zl: (0, 0, 0, 0, 0))
    return pl.pallas_call(
        kernel,
        grid_spec=pltpu.PrefetchScalarGridSpec(
            num_scalar_prefetch=1,
            grid=(pieces // step,),
            in_specs=[a_spec, b_spec, b_spec] + [pl.BlockSpec(m.shape, lambda p, zl: (0, 0)) for m in (turn, pick)],
            out_specs=pl.BlockSpec((step, nx, 2 * rows + EXTRA, LANES), lambda p, zl: (p, 0, 0, 0)),
            scratch_shapes=[pltpu.VMEM((deep, (nx + 1) * 2 * LANES), BF16)],
        ),
        out_shape=jax.ShapeDtypeStruct((pieces, nx, 2 * rows + EXTRA, LANES), BF16),
        compiler_params=pltpu.CompilerParams(vmem_limit_bytes=32 << 20),
        name="multiply",
    )(zl, a, *blocks, jnp.asarray(turn), jnp.asarray(pick))


def finish(parts, row_code, col_code, q):
    pieces, nx, tall, _ = parts.shape
    rows = (tall - EXTRA) // 2
    ncol = col_code.shape[1]
    fold = HALF // 2
    at, to = np.indices((EXTRA, 8))
    turn = onehot(at == to)

    def kernel(p_ref, turn_ref, r_ref, c_ref, o_ref, line):
        for p in range(pieces):
            total = p_ref[p, 0].astype(F32)
            for x in range(1, nx):
                total = total + p_ref[p, x].astype(F32)
            last = dot(total[2 * rows :].astype(BF16), turn_ref[...], (0, 0))
            for parity in range(2):
                for half in range(2):
                    at = ((half * 2 + parity) * pieces + p) * q
                    own = slice(parity * rows, (parity + 1) * rows)
                    for part in range(2):
                        lane = part * HALF + half * fold
                        line[:, at + part * fold : at + (part + 1) * fold] = total[own, lane : lane + fold]
                    col = parity * 2 + half
                    line[:LANES, at + HALF : at + q] = last[:, col : col + 1]
                    line[LANES:, at + HALF : at + q] = last[: rows - LANES, 4 + col : 5 + col]
        kept = r_ref[...] == c_ref[...]
        o_ref[...] = jnp.where(kept, line[...], 0.0).astype(BF16)

    return pl.pallas_call(
        kernel,
        out_shape=jax.ShapeDtypeStruct((rows, ncol), BF16),
        scratch_shapes=[pltpu.VMEM((rows, ncol), F32)],
        compiler_params=pltpu.CompilerParams(vmem_limit_bytes=32 << 20),
        name="finish",
    )(parts, jnp.asarray(turn), row_code, col_code)


def make_shards(ny, nx, nc):
    nzh, nzl = nx * nc * 2, 2
    sort = []
    for s in range(nzh):
        for core in range(nc):
            sort.append((s * nc + core, (s - s % 4 + s % 2 * 2 + core) * nc + s % 4 // 2))
    nz = nzh * nzl
    trade = [(s * nc + core, (s + (1 if s % 2 == core else -1)) % nz * nc + core) for s in range(nz) for core in range(nc)]

    def shards(amplitudes, integrals, occ_irrep, virt_irrep, slab_i, slab_j):
        vir, cblock = amplitudes.shape[1], amplitudes.shape[2]
        nk, q = integrals.shape[0], integrals.shape[2]
        ni = nzh * nzl
        na = vir // (ni * ny)
        zh, zl, y = lax.axis_index("zh"), lax.axis_index("zl"), lax.axis_index("y")
        x, c = lax.axis_index("x"), lax.axis_index("c")

        depth = -(-nk * cblock // LANES) * LANES
        w = pack_columns(integrals.transpose(2, 0, 1).reshape(q, nk * cblock))

        t = amplitudes.reshape(vir // na, na * cblock)
        t, w = lax.optimization_barrier((t, w))
        w = lax.ppermute(w, ("zh", "c"), sort)
        t = lax.all_to_all(t, ("zh", "zl"), 0, 0, tiled=True)
        w = lax.all_gather(w, "zh", axis=0, tiled=True)
        t, w = lax.optimization_barrier((t, w))
        w = w.reshape(nx, 2, nc, SENT, LANES)
        t = lax.all_gather(t, ("y", "c"), axis=0, tiled=True)
        other = lax.ppermute(w, ("zh", "zl", "c"), trade)
        t, other = lax.optimization_barrier((t, other))
        t = order_rows(t, nk, nc, ny, ni, na, cblock, depth)

        parts = multiply(zl.reshape(1), t, [w, other])
        tall = parts.shape[2]
        parts = lax.all_to_all(parts.reshape(ny * nx * tall, LANES), ("y", "x"), 0, 0, tiled=True)
        parts = parts.reshape(ny, nx, tall, LANES)

        a_index = ((zh * nzl + zl) * ny + y) * na + jnp.arange(na, dtype=jnp.int32)
        irr_virt_rows = lookup(virt_irrep, a_index)
        irr_occ_rows = lookup(occ_irrep, slab_i)
        row_code = jnp.bitwise_xor(irr_virt_rows[:, None], irr_occ_rows[None, :]).reshape(na * ni, 1)
        ncol = 2 * nzl * ny * q
        col_index = (x * nc + c) * ncol + jnp.arange(ncol, dtype=jnp.int32)
        irr_occ_cols = lookup(lookup(occ_irrep, slab_j), col_index // vir)
        irr_virt_cols = lookup(virt_irrep, col_index % vir)
        col_code = jnp.bitwise_xor(irr_occ_cols, irr_virt_cols)[None, :]
        out = finish(parts, row_code, col_code, q)
        return out.reshape(na, ni, ncol).transpose(1, 0, 2)

    return shards


def solution(mesh):
    nx, nc, ny = 4, 2, 4
    fine = Mesh(mesh.devices.reshape(nx * nc * 2, 2, ny, nx, nc), ("zh", "zl", "y", "x", "c"))
    row, rep = ("zh", "zl", "y"), ("x", "c")
    return jax.shard_map(
        make_shards(ny, nx, nc),
        mesh=fine,
        in_specs=(P(row, None, rep), P(None, rep, row), P(), P(), P(), P()),
        out_specs=P(None, row, rep),
        check_vma=False,
    )
```

```python
import jax
import jax.numpy as jnp
import numpy as np
from jax import lax
from jax.experimental import pallas as pl
from jax.experimental.pallas import tpu as pltpu
from jax.sharding import Mesh, PartitionSpec as P

BF16 = jnp.bfloat16
F32 = jnp.float32
LANES = 128
HALF = 64
SENT = 176
EXTRA = 16


def lookup(table, index):
    compare = index[:, None] == jnp.arange(table.shape[0], dtype=jnp.int32)[None, :]
    return jnp.sum(jnp.where(compare, table[None, :], 0), axis=1)


def dot(a, b, contract):
    return lax.dot_general(a, b, ((contract[:1], contract[1:]), ((), ())), preferred_element_type=F32)


def onehot(hit):
    return np.asarray(hit).astype(np.dtype(jnp.bfloat16))


def order_rows(gathered, nk, nc, pieces, ni, na, cblock, depth):
    rows = ni * pieces
    to, at = np.indices((rows, rows))
    shuffle = onehot(at == to % ni * pieces + to // ni)
    at, to = np.indices((na * cblock, na * LANES))
    spread = onehot((at // cblock == to // LANES) & (at % cblock == to % LANES))
    at, to = np.indices((nk * LANES, depth))
    pack = onehot((at % LANES < cblock) & (to == at // LANES * cblock + at % LANES))

    def kernel(g_ref, s_ref, t_ref, u_ref, o_ref):
        for core in range(nc):
            wide = []
            for k in range(nk):
                first = (k * nc + core) * rows
                rowed = dot(s_ref[...], g_ref[first : first + rows, :], (1, 0)).astype(BF16)
                wide.append(dot(rowed, t_ref[...], (1, 0)).astype(BF16))
            for a in range(na):
                at = slice(a * LANES, (a + 1) * LANES)
                block = dot(jnp.concatenate([part[:, at] for part in wide], axis=1), u_ref[...], (1, 0))
                block = block.astype(BF16).reshape(pieces, ni, depth)
                o_ref[:, a * ni : (a + 1) * ni, core * depth : (core + 1) * depth] = block

    return pl.pallas_call(
        kernel,
        out_shape=jax.ShapeDtypeStruct((pieces, na * ni, nc * depth), BF16),
        compiler_params=pltpu.CompilerParams(vmem_limit_bytes=32 << 20),
        name="order_rows",
    )(gathered, jnp.asarray(shuffle), jnp.asarray(spread), jnp.asarray(pack))


def pack_columns(w):
    fold = HALF // 2

    def kernel(w_ref, o_ref):
        w = w_ref[...].astype(F32)
        third = w[:HALF, 2 * LANES :]
        third = jnp.concatenate([third[:fold], third[fold:]], axis=1)
        end = w[HALF:, 2 * LANES :]
        last = [w[HALF:, :LANES], w[HALF:, LANES : 2 * LANES], jnp.concatenate([end, jnp.zeros_like(end)], axis=1)]
        last += [jnp.zeros((EXTRA - 3, LANES), F32)]
        packed = [w[:HALF, :LANES], w[:HALF, LANES : 2 * LANES], third, jnp.concatenate(last, axis=0)]
        o_ref[...] = jnp.concatenate(packed, axis=0).astype(BF16)

    return pl.pallas_call(
        kernel,
        out_shape=jax.ShapeDtypeStruct((SENT, LANES), BF16),
        compiler_params=pltpu.CompilerParams(vmem_limit_bytes=32 << 20),
        name="pack_columns",
    )(w)


def multiply(place, a, blocks, came):
    pieces, rows, deep = a.shape
    nx, nc, halves = blocks[0].shape[:3]
    depth = deep // nc
    slots = nx * halves
    step = min(2, pieces)
    fold = HALF // 2
    at, to = np.indices((slots * EXTRA, 3 * LANES))
    turn = onehot((at % EXTRA == to // LANES) & (at // EXTRA == to % LANES))
    to, at = np.indices((nx * EXTRA, 4 * slots))
    x, part, parity, half = to // EXTRA, to % EXTRA // 4, to % 4 // 2, to % 2
    pick = onehot((to % EXTRA < 8) & (at == (part * 2 + parity) * slots + x * halves + half))

    def kernel(place_ref, a_ref, b0, b1, b2, turn_ref, pick_ref, o_ref, cols):
        @pl.when(pl.program_id(0) == 0)
        def _():
            for n in range(2 * nc):
                own_c, own_z = n // 2 == 0, n % 2 == 0
                block_of = lambda x, half, at: (b0, b1)[n % 2][x, 0, half, at, :] if own_c else b2[n % 2, x, half, at, :]
                parity = place_ref[0] if own_z else 1 - place_ref[0]
                core = place_ref[1] if own_c else 1 - place_ref[1]
                first = core * depth
                rows_at = lambda tile: pl.ds(pl.multiple_of(first + tile * LANES, LANES), LANES)
                for x in range(nx):
                    lane = pl.ds(pl.multiple_of((x * 2 + parity) * LANES, LANES), LANES)
                    for tile in range(2):
                        rows_of = [slice(at, at + fold) for at in (tile * HALF, tile * HALF + fold)]
                        block = jnp.concatenate([block_of(x, half, at) for at in rows_of for half in range(halves)], axis=0)
                        cols[rows_at(tile), lane] = block.T
                    block = jnp.concatenate([block_of(x, half, slice(2 * HALF, 2 * HALF + fold)) for half in range(halves)], axis=0)
                    block = block.astype(F32).T
                    block = jnp.concatenate([block[:HALF], block[HALF:]], axis=1)
                    block = jnp.concatenate([block, jnp.zeros_like(block)], axis=0)
                    cols[rows_at(2), lane] = block.astype(BF16)
                lane = pl.ds(pl.multiple_of((nx * 2 + parity) * LANES, LANES), LANES)
                last = jnp.concatenate([block_of(x, half, slice(SENT - EXTRA, SENT)) for x in range(nx) for half in range(halves)], axis=0)
                last = dot(last, turn_ref[...], (0, 0)).astype(BF16)
                for tile in range(3):
                    cols[rows_at(tile), lane] = last[:, tile * LANES : (tile + 1) * LANES]

        out = dot(a_ref[...].reshape(step * rows, deep), cols[...], (1, 0))
        for p in range(step):
            own = out[p * rows : (p + 1) * rows]
            left = [own[:, at * LANES : (at + 1) * LANES].T[:slots] for at in (nx * 2, nx * 2 + 1)]
            blank = jnp.zeros((slots, 2 * LANES - rows), F32)
            left = [part[:, :LANES] for part in left] + [jnp.concatenate([part[:, LANES:], blank], axis=1) for part in left]
            left = dot(pick_ref[...], jnp.concatenate(left, axis=0).astype(BF16), (1, 0)).astype(BF16)
            for x in range(nx):
                for parity in range(2):
                    at = (x * 2 + parity) * LANES
                    o_ref[p, x, parity * rows : (parity + 1) * rows, :] = own[:, at : at + LANES].astype(BF16)
                o_ref[p, x, 2 * rows :, :] = left[x * EXTRA : (x + 1) * EXTRA]

    a_spec = pl.BlockSpec((step, rows, deep), lambda p, place: (p, 0, 0))
    b_spec = pl.BlockSpec((nx, 1, halves, SENT, LANES), lambda p, place: (0, place[1], 0, 0, 0))
    came_spec = pl.BlockSpec(came.shape, lambda p, place: (0, 0, 0, 0, 0))
    return pl.pallas_call(
        kernel,
        grid_spec=pltpu.PrefetchScalarGridSpec(
            num_scalar_prefetch=1,
            grid=(pieces // step,),
            in_specs=[a_spec, b_spec, b_spec, came_spec] + [pl.BlockSpec(m.shape, lambda p, place: (0, 0)) for m in (turn, pick)],
            out_specs=pl.BlockSpec((step, nx, 2 * rows + EXTRA, LANES), lambda p, place: (p, 0, 0, 0)),
            scratch_shapes=[pltpu.VMEM((deep, (nx + 1) * 2 * LANES), BF16)],
        ),
        out_shape=jax.ShapeDtypeStruct((pieces, nx, 2 * rows + EXTRA, LANES), BF16),
        compiler_params=pltpu.CompilerParams(vmem_limit_bytes=32 << 20),
        name="multiply",
    )(place, a, *blocks, came, jnp.asarray(turn), jnp.asarray(pick))


def finish(parts, row_code, col_code, q):
    pieces, nx, tall, _ = parts.shape
    rows = (tall - EXTRA) // 2
    ncol = col_code.shape[1]
    fold = HALF // 2
    at, to = np.indices((EXTRA, 8))
    turn = onehot(at == to)

    def kernel(p_ref, turn_ref, r_ref, c_ref, o_ref, line):
        for p in range(pieces):
            total = p_ref[p, 0].astype(F32)
            for x in range(1, nx):
                total = total + p_ref[p, x].astype(F32)
            last = dot(total[2 * rows :].astype(BF16), turn_ref[...], (0, 0))
            for parity in range(2):
                for half in range(2):
                    at = ((half * 2 + parity) * pieces + p) * q
                    own = slice(parity * rows, (parity + 1) * rows)
                    for part in range(2):
                        lane = part * HALF + half * fold
                        line[:, at + part * fold : at + (part + 1) * fold] = total[own, lane : lane + fold]
                    col = parity * 2 + half
                    line[:LANES, at + HALF : at + q] = last[:, col : col + 1]
                    line[LANES:, at + HALF : at + q] = last[: rows - LANES, 4 + col : 5 + col]
        kept = r_ref[...] == c_ref[...]
        o_ref[...] = jnp.where(kept, line[...], 0.0).astype(BF16)

    return pl.pallas_call(
        kernel,
        out_shape=jax.ShapeDtypeStruct((rows, ncol), BF16),
        scratch_shapes=[pltpu.VMEM((rows, ncol), F32)],
        compiler_params=pltpu.CompilerParams(vmem_limit_bytes=32 << 20),
        name="finish",
    )(parts, jnp.asarray(turn), row_code, col_code)


def make_shards(ny, nx, nc):
    nzh, nzl = nx * nc * 2, 2
    nz = nzh * nzl
    swap = [(0, 1), (1, 0)]
    trade = [(s * nc + core, (s + (1 if s % 2 == core else -1)) % nz * nc + core) for s in range(nz) for core in range(nc)]

    def shards(amplitudes, integrals, occ_irrep, virt_irrep, slab_i, slab_j):
        vir, cblock = amplitudes.shape[1], amplitudes.shape[2]
        nk, q = integrals.shape[0], integrals.shape[2]
        ni = nzh * nzl
        na = vir // (ni * ny)
        zh, zl, y = lax.axis_index("zh"), lax.axis_index("zl"), lax.axis_index("y")
        x, c = lax.axis_index("x"), lax.axis_index("c")

        depth = -(-nk * cblock // LANES) * LANES
        w = pack_columns(integrals.transpose(2, 0, 1).reshape(q, nk * cblock))

        t = amplitudes.reshape(vir // na, na * cblock)
        t = lax.all_to_all(t, ("zh", "zl"), 0, 0, tiled=True)
        w = lax.all_gather(w, "zh", axis=0, tiled=True)
        t, w = lax.optimization_barrier((t, w))
        w = w.reshape(nx, nc, 2, SENT, LANES)
        t = lax.all_gather(t, ("y", "c"), axis=0, tiled=True)
        other = lax.ppermute(w, ("zh", "zl", "c"), trade)
        t, other = lax.optimization_barrier((t, other))
        given = [lax.dynamic_index_in_dim(part, 1 - c, 1, keepdims=False) for part in (w, other)]
        came = lax.ppermute(jnp.stack(given), "c", swap)
        t = order_rows(t, nk, nc, ny, ni, na, cblock, depth)

        parts = multiply(jnp.stack([zl, c]), t, [w, other], came)
        tall = parts.shape[2]
        parts = lax.all_to_all(parts.reshape(ny * nx * tall, LANES), ("y", "x"), 0, 0, tiled=True)
        parts = parts.reshape(ny, nx, tall, LANES)

        a_index = ((zh * nzl + zl) * ny + y) * na + jnp.arange(na, dtype=jnp.int32)
        irr_virt_rows = lookup(virt_irrep, a_index)
        irr_occ_rows = lookup(occ_irrep, slab_i)
        row_code = jnp.bitwise_xor(irr_virt_rows[:, None], irr_occ_rows[None, :]).reshape(na * ni, 1)
        ncol = 2 * nzl * ny * q
        col_index = (x * nc + c) * ncol + jnp.arange(ncol, dtype=jnp.int32)
        irr_occ_cols = lookup(lookup(occ_irrep, slab_j), col_index // vir)
        irr_virt_cols = lookup(virt_irrep, col_index % vir)
        col_code = jnp.bitwise_xor(irr_occ_cols, irr_virt_cols)[None, :]
        out = finish(parts, row_code, col_code, q)
        return out.reshape(na, ni, ncol).transpose(1, 0, 2)

    return shards


def solution(mesh):
    nx, nc, ny = 4, 2, 4
    fine = Mesh(mesh.devices.reshape(nx * nc * 2, 2, ny, nx, nc), ("zh", "zl", "y", "x", "c"))
    row, rep = ("zh", "zl", "y"), ("x", "c")
    return jax.shard_map(
        make_shards(ny, nx, nc),
        mesh=fine,
        in_specs=(P(row, None, rep), P(None, rep, row), P(), P(), P(), P()),
        out_specs=P(None, row, rep),
        check_vma=False,
    )
```

```python
import jax
import jax.numpy as jnp
import numpy as np
from jax import lax
from jax.experimental import pallas as pl
from jax.experimental.pallas import tpu as pltpu
from jax.sharding import Mesh, PartitionSpec as P

BF16 = jnp.bfloat16
F32 = jnp.float32
LANES = 128
HALF = 64
SENT = 176
EXTRA = 16


def lookup(table, index):
    compare = index[:, None] == jnp.arange(table.shape[0], dtype=jnp.int32)[None, :]
    return jnp.sum(jnp.where(compare, table[None, :], 0), axis=1)


def dot(a, b, contract):
    return lax.dot_general(a, b, ((contract[:1], contract[1:]), ((), ())), preferred_element_type=F32)


def onehot(hit):
    return np.asarray(hit).astype(np.dtype(jnp.bfloat16))


def order_rows(gathered, nk, nc, pieces, ni, na, cblock, depth):
    rows = ni * pieces
    to, at = np.indices((rows, rows))
    shuffle = onehot(at == to % ni * pieces + to // ni)

    def kernel(g_ref, s_ref, o_ref):
        blank = jnp.zeros((rows, depth - nk * cblock), F32)
        for core in range(nc):
            parts = []
            for k in range(nk):
                first = (k * nc + core) * rows
                parts.append(dot(s_ref[...], g_ref[first : first + rows, :], (1, 0)))
            for a in range(na):
                at = slice(a * cblock, (a + 1) * cblock)
                block = jnp.concatenate([part[:, at] for part in parts] + [blank], axis=1)
                block = block.astype(BF16).reshape(pieces, ni, depth)
                o_ref[:, a * ni : (a + 1) * ni, core * depth : (core + 1) * depth] = block

    return pl.pallas_call(
        kernel,
        out_shape=jax.ShapeDtypeStruct((pieces, na * ni, nc * depth), BF16),
        compiler_params=pltpu.CompilerParams(vmem_limit_bytes=32 << 20),
        name="order_rows",
    )(gathered, jnp.asarray(shuffle))


def pack_columns(w):
    fold = HALF // 2

    def kernel(w_ref, o_ref):
        w = w_ref[...].astype(F32)
        third = w[:HALF, 2 * LANES :]
        third = jnp.concatenate([third[:fold], third[fold:]], axis=1)
        end = w[HALF:, 2 * LANES :]
        last = [w[HALF:, :LANES], w[HALF:, LANES : 2 * LANES], jnp.concatenate([end, jnp.zeros_like(end)], axis=1)]
        last += [jnp.zeros((EXTRA - 3, LANES), F32)]
        packed = [w[:HALF, :LANES], w[:HALF, LANES : 2 * LANES], third, jnp.concatenate(last, axis=0)]
        o_ref[...] = jnp.concatenate(packed, axis=0).astype(BF16)

    return pl.pallas_call(
        kernel,
        out_shape=jax.ShapeDtypeStruct((SENT, LANES), BF16),
        compiler_params=pltpu.CompilerParams(vmem_limit_bytes=32 << 20),
        name="pack_columns",
    )(w)


def multiply(place, a, blocks, came):
    pieces, rows, deep = a.shape
    nx, nc, halves = blocks[0].shape[:3]
    depth = deep // nc
    slots = nx * halves
    fold = HALF // 2
    to, at = np.indices((3 * EXTRA, slots * EXTRA))
    turn = onehot((at % EXTRA == to // EXTRA) & (at // EXTRA == to % EXTRA))
    to, at = np.indices((nx * EXTRA, 4 * slots))
    x, part, parity, half = to // EXTRA, to % EXTRA // 4, to % 4 // 2, to % 2
    pick = onehot((to % EXTRA < 8) & (at == (part * 2 + parity) * slots + x * halves + half))

    def kernel(place_ref, a_ref, b0, b1, b2, turn_ref, pick_ref, o_ref, cols):
        for n in range(2 * nc):
            own_c, own_z = n // 2 == 0, n % 2 == 0
            block_of = lambda x, half, at: (b0, b1)[n % 2][x, place_ref[1], half, at, :] if own_c else b2[n % 2, x, half, at, :]
            parity = place_ref[0] if own_z else 1 - place_ref[0]
            core = place_ref[1] if own_c else 1 - place_ref[1]
            lanes = [pl.ds(pl.multiple_of(core * depth + tile * LANES, LANES), LANES) for tile in range(3)]
            for x in range(nx):
                for half in range(halves):
                    first = pl.multiple_of(((x * 2 + parity) * halves + half) * HALF, HALF)
                    for tile in range(2):
                        cols[pl.ds(first, HALF), lanes[tile]] = block_of(x, half, slice(tile * HALF, (tile + 1) * HALF))
                    third = block_of(x, half, slice(2 * HALF, 2 * HALF + fold)).astype(F32)
                    third = jnp.concatenate([third[:, :HALF], third[:, HALF:]], axis=0)
                    cols[pl.ds(first, HALF), lanes[2]] = jnp.concatenate([third, jnp.zeros_like(third)], axis=1).astype(BF16)
            last = jnp.concatenate([block_of(x, half, slice(SENT - EXTRA, SENT)) for x in range(nx) for half in range(halves)], axis=0)
            last = dot(turn_ref[...], last, (1, 0)).astype(BF16)
            first = pl.multiple_of(nx * 2 * LANES + parity * EXTRA, EXTRA)
            for tile in range(3):
                cols[pl.ds(first, EXTRA), lanes[tile]] = last[tile * EXTRA : (tile + 1) * EXTRA]

        a = a_ref[...].reshape(pieces * rows, deep)
        for x in range(nx):
            out = dot(a, cols[x * 2 * LANES : (x + 1) * 2 * LANES, :], (1, 1)).astype(BF16)
            for p in range(pieces):
                for parity in range(2):
                    own = out[p * rows : (p + 1) * rows, parity * LANES : (parity + 1) * LANES]
                    o_ref[p, x, parity * rows : (parity + 1) * rows, :] = own
        blank = jnp.zeros((slots, 2 * LANES - rows), F32)
        for p in range(pieces):
            last = dot(cols[nx * 2 * LANES :, :], a_ref[p], (1, 1))
            left = [last[at * EXTRA : at * EXTRA + slots] for at in range(2)]
            left = [part[:, :LANES] for part in left] + [jnp.concatenate([part[:, LANES:], blank], axis=1) for part in left]
            left = dot(pick_ref[...], jnp.concatenate(left, axis=0).astype(BF16), (1, 0)).astype(BF16)
            for x in range(nx):
                o_ref[p, x, 2 * rows :, :] = left[x * EXTRA : (x + 1) * EXTRA]

    whole = pl.BlockSpec(memory_space=pltpu.VMEM)
    return pl.pallas_call(
        kernel,
        in_specs=[pl.BlockSpec(memory_space=pltpu.SMEM)] + [whole] * 6,
        out_specs=whole,
        scratch_shapes=[pltpu.VMEM((nx * 2 * LANES + 2 * EXTRA, deep), BF16)],
        out_shape=jax.ShapeDtypeStruct((pieces, nx, 2 * rows + EXTRA, LANES), BF16),
        compiler_params=pltpu.CompilerParams(vmem_limit_bytes=32 << 20),
        name="multiply",
    )(place, a, *blocks, came, jnp.asarray(turn), jnp.asarray(pick))


def finish(parts, row_code, col_code, q):
    pieces, nx, tall, _ = parts.shape
    rows = (tall - EXTRA) // 2
    ncol = col_code.shape[1]
    at, to = np.indices((EXTRA, 8))
    turn = onehot(at == to)

    def kernel(p_ref, turn_ref, r_ref, c_ref, o_ref, line):
        for p in range(pieces):
            total = p_ref[p, 0].astype(F32)
            for x in range(1, nx):
                total = total + p_ref[p, x].astype(F32)
            last = dot(total[2 * rows :].astype(BF16), turn_ref[...], (0, 0))
            for parity in range(2):
                for half in range(2):
                    at = ((half * 2 + parity) * pieces + p) * q
                    own = slice(parity * rows, (parity + 1) * rows)
                    line[:, at : at + HALF] = total[own, half * HALF : (half + 1) * HALF]
                    col = parity * 2 + half
                    line[:LANES, at + HALF : at + q] = last[:, col : col + 1]
                    line[LANES:, at + HALF : at + q] = last[: rows - LANES, 4 + col : 5 + col]
        kept = r_ref[...] == c_ref[...]
        o_ref[...] = jnp.where(kept, line[...], 0.0).astype(BF16)

    return pl.pallas_call(
        kernel,
        out_shape=jax.ShapeDtypeStruct((rows, ncol), BF16),
        scratch_shapes=[pltpu.VMEM((rows, ncol), F32)],
        compiler_params=pltpu.CompilerParams(vmem_limit_bytes=32 << 20),
        name="finish",
    )(parts, jnp.asarray(turn), row_code, col_code)


def make_shards(ny, nx, nc):
    nzh, nzl = nx * nc * 2, 2
    nz = nzh * nzl
    swap = [(0, 1), (1, 0)]
    trade = [(s * nc + core, (s + (1 if s % 2 == core else -1)) % nz * nc + core) for s in range(nz) for core in range(nc)]

    def shards(amplitudes, integrals, occ_irrep, virt_irrep, slab_i, slab_j):
        vir, cblock = amplitudes.shape[1], amplitudes.shape[2]
        nk, q = integrals.shape[0], integrals.shape[2]
        ni = nzh * nzl
        na = vir // (ni * ny)
        zh, zl, y = lax.axis_index("zh"), lax.axis_index("zl"), lax.axis_index("y")
        x, c = lax.axis_index("x"), lax.axis_index("c")

        depth = -(-nk * cblock // LANES) * LANES
        w = pack_columns(integrals.transpose(2, 0, 1).reshape(q, nk * cblock))

        t = amplitudes.reshape(vir // na, na * cblock)
        t = lax.all_to_all(t, ("zh", "zl"), 0, 0, tiled=True)
        w = lax.all_gather(w, "zh", axis=0, tiled=True)
        t, w = lax.optimization_barrier((t, w))
        w = w.reshape(nx, nc, 2, SENT, LANES)
        t = lax.all_gather(t, ("y", "c"), axis=0, tiled=True)
        other = lax.ppermute(w, ("zh", "zl", "c"), trade)
        t, other = lax.optimization_barrier((t, other))
        given = [lax.dynamic_index_in_dim(part, 1 - c, 1, keepdims=False) for part in (w, other)]
        came = lax.ppermute(jnp.stack(given), "c", swap)
        t = order_rows(t, nk, nc, ny, ni, na, cblock, depth)

        parts = multiply(jnp.stack([zl, c]), t, [w, other], came)
        tall = parts.shape[2]
        parts = lax.all_to_all(parts.reshape(ny * nx * tall, LANES), ("y", "x"), 0, 0, tiled=True)
        parts = parts.reshape(ny, nx, tall, LANES)

        a_index = ((zh * nzl + zl) * ny + y) * na + jnp.arange(na, dtype=jnp.int32)
        irr_virt_rows = lookup(virt_irrep, a_index)
        irr_occ_rows = lookup(occ_irrep, slab_i)
        row_code = jnp.bitwise_xor(irr_virt_rows[:, None], irr_occ_rows[None, :]).reshape(na * ni, 1)
        ncol = 2 * nzl * ny * q
        col_index = (x * nc + c) * ncol + jnp.arange(ncol, dtype=jnp.int32)
        irr_occ_cols = lookup(lookup(occ_irrep, slab_j), col_index // vir)
        irr_virt_cols = lookup(virt_irrep, col_index % vir)
        col_code = jnp.bitwise_xor(irr_occ_cols, irr_virt_cols)[None, :]
        out = finish(parts, row_code, col_code, q)
        return out.reshape(na, ni, ncol).transpose(1, 0, 2)

    return shards


def solution(mesh):
    nx, nc, ny = 4, 2, 4
    fine = Mesh(mesh.devices.reshape(nx * nc * 2, 2, ny, nx, nc), ("zh", "zl", "y", "x", "c"))
    row, rep = ("zh", "zl", "y"), ("x", "c")
    return jax.shard_map(
        make_shards(ny, nx, nc),
        mesh=fine,
        in_specs=(P(row, None, rep), P(None, rep, row), P(), P(), P(), P()),
        out_specs=P(None, row, rep),
        check_vma=False,
    )
```

```python
import jax
import jax.numpy as jnp
import numpy as np
from jax import lax
from jax.experimental import pallas as pl
from jax.experimental.pallas import tpu as pltpu
from jax.sharding import Mesh, PartitionSpec as P

BF16 = jnp.bfloat16
F32 = jnp.float32
LANES = 128
HALF = 64
SENT = 176
EXTRA = 16


def lookup(table, index):
    compare = index[:, None] == jnp.arange(table.shape[0], dtype=jnp.int32)[None, :]
    return jnp.sum(jnp.where(compare, table[None, :], 0), axis=1)


def dot(a, b, contract):
    return lax.dot_general(a, b, ((contract[:1], contract[1:]), ((), ())), preferred_element_type=F32)


def onehot(hit):
    return np.asarray(hit).astype(np.dtype(jnp.bfloat16))


def order_rows(gathered, nk, nc, pieces, ni, na, cblock, depth):
    rows, part = ni * pieces, cblock // 2
    to, at = np.indices((2 * rows, 2 * rows))
    shuffle = onehot(at == (to % ni * pieces + to % rows // ni) * 2 + to // rows)

    def kernel(g_ref, s_ref, o_ref):
        blank = jnp.zeros((rows, depth - nk * cblock), F32)
        for core in range(nc):
            parts = []
            for k in range(nk):
                first = (k * nc + core) * 2 * rows
                both = dot(s_ref[...], g_ref[first : first + 2 * rows, :], (1, 0))
                parts += [both[:rows], both[rows:]]
            for a in range(na):
                at = slice(a * part, (a + 1) * part)
                block = jnp.concatenate([one[:, at] for one in parts] + [blank], axis=1)
                block = block.astype(BF16).reshape(pieces, ni, depth)
                o_ref[:, a * ni : (a + 1) * ni, core * depth : (core + 1) * depth] = block

    return pl.pallas_call(
        kernel,
        out_shape=jax.ShapeDtypeStruct((pieces, na * ni, nc * depth), BF16),
        compiler_params=pltpu.CompilerParams(vmem_limit_bytes=32 << 20),
        name="order_rows",
    )(gathered, jnp.asarray(shuffle))


def prepare(x, w, na):
    cblock, vir = x.shape
    rows, part, nk = vir // na, cblock // 2, w.shape[1]
    fold = HALF // 2

    def kernel(x_ref, w_ref, t_ref, o_ref, tall, left, right):
        tall[:, :cblock] = x_ref[...].astype(F32).T
        every = [tall[pl.ds(a, rows, stride=na), :] for a in range(na)]
        for half in range(2):
            at = slice(half * part, (half + 1) * part)
            blank = jnp.zeros((rows, 2 * LANES - na * part), F32)
            line = jnp.concatenate([one[:, at] for one in every] + [blank], axis=1)
            left[pl.ds(half, rows, stride=2), :] = line[:, :LANES]
            right[pl.ds(half, rows, stride=2), :] = line[:, LANES:]
        t_ref[:, :LANES] = left[...].astype(BF16)
        t_ref[:, LANES:] = right[:, : na * part - LANES].astype(BF16)

        w = w_ref[...].astype(F32)
        w = jnp.concatenate([w[:, k, :] for k in range(nk)], axis=1)
        third = w[:HALF, 2 * LANES :]
        third = jnp.concatenate([third[:fold], third[fold:]], axis=1)
        end = w[HALF:, 2 * LANES :]
        last = [w[HALF:, :LANES], w[HALF:, LANES : 2 * LANES], jnp.concatenate([end, jnp.zeros_like(end)], axis=1)]
        last += [jnp.zeros((EXTRA - 3, LANES), F32)]
        packed = [w[:HALF, :LANES], w[:HALF, LANES : 2 * LANES], third, jnp.concatenate(last, axis=0)]
        o_ref[...] = jnp.concatenate(packed, axis=0).astype(BF16)

    return pl.pallas_call(
        kernel,
        out_shape=[jax.ShapeDtypeStruct((2 * rows, na * part), BF16), jax.ShapeDtypeStruct((SENT, LANES), BF16)],
        scratch_shapes=[pltpu.VMEM((tall, LANES), F32) for tall in (vir, 2 * rows, 2 * rows)],
        compiler_params=pltpu.CompilerParams(vmem_limit_bytes=32 << 20),
        name="prepare",
    )(x, w)


def multiply(place, a, blocks, came):
    pieces, rows, deep = a.shape
    nx, nc, halves = blocks[0].shape[:3]
    depth = deep // nc
    slots = nx * halves
    fold = HALF // 2
    to, at = np.indices((3 * EXTRA, slots * EXTRA))
    turn = onehot((at % EXTRA == to // EXTRA) & (at // EXTRA == to % EXTRA))
    to, at = np.indices((nx * EXTRA, 4 * slots))
    x, part, parity, half = to // EXTRA, to % EXTRA // 4, to % 4 // 2, to % 2
    pick = onehot((to % EXTRA < 8) & (at == (part * 2 + parity) * slots + x * halves + half))

    def kernel(place_ref, a_ref, b0, b1, b2, turn_ref, pick_ref, o_ref, cols):
        for n in range(2 * nc):
            own_c, own_z = n // 2 == 0, n % 2 == 0
            block_of = lambda x, half, at: (b0, b1)[n % 2][x, place_ref[1], half, at, :] if own_c else b2[n % 2, x, half, at, :]
            parity = place_ref[0] if own_z else 1 - place_ref[0]
            core = place_ref[1] if own_c else 1 - place_ref[1]
            lanes = [pl.ds(pl.multiple_of(core * depth + tile * LANES, LANES), LANES) for tile in range(3)]
            for x in range(nx):
                for half in range(halves):
                    first = pl.multiple_of(((x * 2 + parity) * halves + half) * HALF, HALF)
                    for tile in range(2):
                        cols[pl.ds(first, HALF), lanes[tile]] = block_of(x, half, slice(tile * HALF, (tile + 1) * HALF))
                    third = block_of(x, half, slice(2 * HALF, 2 * HALF + fold)).astype(F32)
                    third = jnp.concatenate([third[:, :HALF], third[:, HALF:]], axis=0)
                    cols[pl.ds(first, HALF), lanes[2]] = jnp.concatenate([third, jnp.zeros_like(third)], axis=1).astype(BF16)
            last = jnp.concatenate([block_of(x, half, slice(SENT - EXTRA, SENT)) for x in range(nx) for half in range(halves)], axis=0)
            last = dot(turn_ref[...], last, (1, 0)).astype(BF16)
            first = pl.multiple_of(nx * 2 * LANES + parity * EXTRA, EXTRA)
            for tile in range(3):
                cols[pl.ds(first, EXTRA), lanes[tile]] = last[tile * EXTRA : (tile + 1) * EXTRA]

        a = a_ref[...].reshape(pieces * rows, deep)
        for x in range(nx):
            out = dot(a, cols[x * 2 * LANES : (x + 1) * 2 * LANES, :], (1, 1)).astype(BF16)
            for p in range(pieces):
                for parity in range(2):
                    own = out[p * rows : (p + 1) * rows, parity * LANES : (parity + 1) * LANES]
                    o_ref[p, x, parity * rows : (parity + 1) * rows, :] = own
        blank = jnp.zeros((slots, 2 * LANES - rows), F32)
        for p in range(pieces):
            last = dot(cols[nx * 2 * LANES :, :], a_ref[p], (1, 1))
            left = [last[at * EXTRA : at * EXTRA + slots] for at in range(2)]
            left = [part[:, :LANES] for part in left] + [jnp.concatenate([part[:, LANES:], blank], axis=1) for part in left]
            left = dot(pick_ref[...], jnp.concatenate(left, axis=0).astype(BF16), (1, 0)).astype(BF16)
            for x in range(nx):
                o_ref[p, x, 2 * rows :, :] = left[x * EXTRA : (x + 1) * EXTRA]

    whole = pl.BlockSpec(memory_space=pltpu.VMEM)
    return pl.pallas_call(
        kernel,
        in_specs=[pl.BlockSpec(memory_space=pltpu.SMEM)] + [whole] * 6,
        out_specs=whole,
        scratch_shapes=[pltpu.VMEM((nx * 2 * LANES + 2 * EXTRA, deep), BF16)],
        out_shape=jax.ShapeDtypeStruct((pieces, nx, 2 * rows + EXTRA, LANES), BF16),
        compiler_params=pltpu.CompilerParams(vmem_limit_bytes=32 << 20),
        name="multiply",
    )(place, a, *blocks, came, jnp.asarray(turn), jnp.asarray(pick))


def finish(parts, row_code, col_code, q):
    pieces, nx, tall, _ = parts.shape
    rows = (tall - EXTRA) // 2
    ncol = col_code.shape[1]
    at, to = np.indices((EXTRA, 8))
    turn = onehot(at == to)

    def kernel(p_ref, turn_ref, r_ref, c_ref, o_ref, line):
        for p in range(pieces):
            total = p_ref[p, 0].astype(F32)
            for x in range(1, nx):
                total = total + p_ref[p, x].astype(F32)
            last = dot(total[2 * rows :].astype(BF16), turn_ref[...], (0, 0))
            for parity in range(2):
                for half in range(2):
                    at = ((half * 2 + parity) * pieces + p) * q
                    own = slice(parity * rows, (parity + 1) * rows)
                    line[:, at : at + HALF] = total[own, half * HALF : (half + 1) * HALF]
                    col = parity * 2 + half
                    line[:LANES, at + HALF : at + q] = last[:, col : col + 1]
                    line[LANES:, at + HALF : at + q] = last[: rows - LANES, 4 + col : 5 + col]
        kept = r_ref[...] == c_ref[...]
        o_ref[...] = jnp.where(kept, line[...], 0.0).astype(BF16)

    return pl.pallas_call(
        kernel,
        out_shape=jax.ShapeDtypeStruct((rows, ncol), BF16),
        scratch_shapes=[pltpu.VMEM((rows, ncol), F32)],
        compiler_params=pltpu.CompilerParams(vmem_limit_bytes=32 << 20),
        name="finish",
    )(parts, jnp.asarray(turn), row_code, col_code)


def make_shards(ny, nx, nc):
    nzh, nzl = nx * nc * 2, 2
    nz = nzh * nzl
    swap = [(0, 1), (1, 0)]
    trade = [(s * nc + core, (s + (1 if s % 2 == core else -1)) % nz * nc + core) for s in range(nz) for core in range(nc)]

    def shards(amplitudes, integrals, occ_irrep, virt_irrep, slab_i, slab_j):
        vir, cblock = amplitudes.shape[1], amplitudes.shape[2]
        nk, q = integrals.shape[0], integrals.shape[2]
        ni = nzh * nzl
        na = vir // (ni * ny)
        zh, zl, y = lax.axis_index("zh"), lax.axis_index("zl"), lax.axis_index("y")
        x, c = lax.axis_index("x"), lax.axis_index("c")

        depth = -(-nk * cblock // LANES) * LANES
        t, w = prepare(amplitudes.reshape(vir, cblock).T, integrals.transpose(2, 0, 1), na)

        t = lax.all_to_all(t, ("zh", "zl"), 0, 0, tiled=True)
        w = lax.all_gather(w, "zh", axis=0, tiled=True)
        t, w = lax.optimization_barrier((t, w))
        w = w.reshape(nx, nc, 2, SENT, LANES)
        t = lax.all_gather(t, ("y", "c"), axis=0, tiled=True)
        other = lax.ppermute(w, ("zh", "zl", "c"), trade)
        t, other = lax.optimization_barrier((t, other))
        given = [lax.dynamic_index_in_dim(part, 1 - c, 1, keepdims=False) for part in (w, other)]
        came = lax.ppermute(jnp.stack(given), "c", swap)
        t = order_rows(t, nk, nc, ny, ni, na, cblock, depth)

        parts = multiply(jnp.stack([zl, c]), t, [w, other], came)
        tall = parts.shape[2]
        parts = lax.all_to_all(parts.reshape(ny * nx * tall, LANES), ("y", "x"), 0, 0, tiled=True)
        parts = parts.reshape(ny, nx, tall, LANES)

        a_index = ((zh * nzl + zl) * ny + y) * na + jnp.arange(na, dtype=jnp.int32)
        irr_virt_rows = lookup(virt_irrep, a_index)
        irr_occ_rows = lookup(occ_irrep, slab_i)
        row_code = jnp.bitwise_xor(irr_virt_rows[:, None], irr_occ_rows[None, :]).reshape(na * ni, 1)
        ncol = 2 * nzl * ny * q
        col_index = (x * nc + c) * ncol + jnp.arange(ncol, dtype=jnp.int32)
        irr_occ_cols = lookup(lookup(occ_irrep, slab_j), col_index // vir)
        irr_virt_cols = lookup(virt_irrep, col_index % vir)
        col_code = jnp.bitwise_xor(irr_occ_cols, irr_virt_cols)[None, :]
        out = finish(parts, row_code, col_code, q)
        return out.reshape(na, ni, ncol).transpose(1, 0, 2)

    return shards


def solution(mesh):
    nx, nc, ny = 4, 2, 4
    fine = Mesh(mesh.devices.reshape(nx * nc * 2, 2, ny, nx, nc), ("zh", "zl", "y", "x", "c"))
    row, rep = ("zh", "zl", "y"), ("x", "c")
    return jax.shard_map(
        make_shards(ny, nx, nc),
        mesh=fine,
        in_specs=(P(row, None, rep), P(None, rep, row), P(), P(), P(), P()),
        out_specs=P(None, row, rep),
        check_vma=False,
    )
```

```python
import jax
import jax.numpy as jnp
import numpy as np
from jax import lax
from jax.experimental import pallas as pl
from jax.experimental.pallas import tpu as pltpu
from jax.sharding import Mesh, PartitionSpec as P

BF16 = jnp.bfloat16
F32 = jnp.float32
LANES = 128
HALF = 64
SENT = 176
EXTRA = 16


def lookup(table, index):
    compare = index[:, None] == jnp.arange(table.shape[0], dtype=jnp.int32)[None, :]
    return jnp.sum(jnp.where(compare, table[None, :], 0), axis=1)


def dot(a, b, contract):
    return lax.dot_general(a, b, ((contract[:1], contract[1:]), ((), ())), preferred_element_type=F32)


def onehot(hit):
    return np.asarray(hit).astype(np.dtype(jnp.bfloat16))


def order_rows(gathered, nk, nc, pieces, ni, na, cblock, depth):
    rows = ni * pieces
    to, at = np.indices((rows, rows))
    shuffle = onehot(at == to % ni * pieces + to // ni)

    def kernel(g_ref, s_ref, o_ref):
        blank = jnp.zeros((rows, depth - nk * cblock), F32)
        for core in range(nc):
            parts = []
            for k in range(nk):
                first = (k * nc + core) * rows
                parts.append(dot(s_ref[...], g_ref[first : first + rows, :], (1, 0)))
            for a in range(na):
                at = slice(a * cblock, (a + 1) * cblock)
                block = jnp.concatenate([part[:, at] for part in parts] + [blank], axis=1)
                block = block.astype(BF16).reshape(pieces, ni, depth)
                o_ref[:, a * ni : (a + 1) * ni, core * depth : (core + 1) * depth] = block

    return pl.pallas_call(
        kernel,
        out_shape=jax.ShapeDtypeStruct((pieces, na * ni, nc * depth), BF16),
        compiler_params=pltpu.CompilerParams(vmem_limit_bytes=32 << 20),
        name="order_rows",
    )(gathered, jnp.asarray(shuffle))


def pack_columns(w):
    fold = HALF // 2

    def kernel(w_ref, o_ref):
        w = w_ref[...].astype(F32)
        third = w[:HALF, 2 * LANES :]
        third = jnp.concatenate([third[:fold], third[fold:]], axis=1)
        end = w[HALF:, 2 * LANES :]
        last = [w[HALF:, :LANES], w[HALF:, LANES : 2 * LANES], jnp.concatenate([end, jnp.zeros_like(end)], axis=1)]
        last += [jnp.zeros((EXTRA - 3, LANES), F32)]
        packed = [w[:HALF, :LANES], w[:HALF, LANES : 2 * LANES], third, jnp.concatenate(last, axis=0)]
        o_ref[...] = jnp.concatenate(packed, axis=0).astype(BF16)

    return pl.pallas_call(
        kernel,
        out_shape=jax.ShapeDtypeStruct((SENT, LANES), BF16),
        compiler_params=pltpu.CompilerParams(vmem_limit_bytes=32 << 20),
        name="pack_columns",
    )(w)


def multiply(place, a, blocks, came):
    pieces, rows, deep = a.shape
    nx, nc, halves = blocks[0].shape[:3]
    depth = deep // nc
    slots = nx * halves
    fold = HALF // 2
    to, at = np.indices((3 * EXTRA, slots * EXTRA))
    turn = onehot((at % EXTRA == to // EXTRA) & (at // EXTRA == to % EXTRA))
    to, at = np.indices((nx * EXTRA, 4 * slots))
    x, part, parity, half = to // EXTRA, to % EXTRA // 4, to % 4 // 2, to % 2
    pick = onehot((to % EXTRA < 8) & (at == (part * 2 + parity) * slots + x * halves + half))

    def kernel(place_ref, a_ref, b0, b1, b2, turn_ref, pick_ref, o_ref, cols):
        for n in range(2 * nc):
            own_c, own_z = n // 2 == 0, n % 2 == 0
            block_of = lambda x, half, at: (b0, b1)[n % 2][x, place_ref[1], half, at, :] if own_c else b2[n % 2, x, half, at, :]
            parity = place_ref[0] if own_z else 1 - place_ref[0]
            core = place_ref[1] if own_c else 1 - place_ref[1]
            lanes = [pl.ds(pl.multiple_of(core * depth + tile * LANES, LANES), LANES) for tile in range(3)]
            for x in range(nx):
                for half in range(halves):
                    first = pl.multiple_of(((x * 2 + parity) * halves + half) * HALF, HALF)
                    for tile in range(2):
                        cols[pl.ds(first, HALF), lanes[tile]] = block_of(x, half, slice(tile * HALF, (tile + 1) * HALF))
                    third = block_of(x, half, slice(2 * HALF, 2 * HALF + fold)).astype(F32)
                    third = jnp.concatenate([third[:, :HALF], third[:, HALF:]], axis=0)
                    cols[pl.ds(first, HALF), lanes[2]] = jnp.concatenate([third, jnp.zeros_like(third)], axis=1).astype(BF16)
            last = jnp.concatenate([block_of(x, half, slice(SENT - EXTRA, SENT)) for x in range(nx) for half in range(halves)], axis=0)
            last = dot(turn_ref[...], last, (1, 0)).astype(BF16)
            first = pl.multiple_of(nx * 2 * LANES + parity * EXTRA, EXTRA)
            for tile in range(3):
                cols[pl.ds(first, EXTRA), lanes[tile]] = last[tile * EXTRA : (tile + 1) * EXTRA]

        a = a_ref[...].reshape(pieces * rows, deep)
        for x in range(nx):
            out = dot(a, cols[x * 2 * LANES : (x + 1) * 2 * LANES, :], (1, 1)).astype(BF16)
            for p in range(pieces):
                for parity in range(2):
                    own = out[p * rows : (p + 1) * rows, parity * LANES : (parity + 1) * LANES]
                    o_ref[x, p, parity * rows : (parity + 1) * rows, :] = own
        blank = jnp.zeros((slots, 2 * LANES - rows), F32)
        every = dot(a, cols[nx * 2 * LANES :, :], (1, 1))
        for p in range(pieces):
            last = every[p * rows : (p + 1) * rows].T
            left = [last[at * EXTRA : at * EXTRA + slots] for at in range(2)]
            left = [part[:, :LANES] for part in left] + [jnp.concatenate([part[:, LANES:], blank], axis=1) for part in left]
            left = dot(pick_ref[...], jnp.concatenate(left, axis=0).astype(BF16), (1, 0)).astype(BF16)
            for x in range(nx):
                o_ref[x, p, 2 * rows :, :] = left[x * EXTRA : (x + 1) * EXTRA]

    whole = pl.BlockSpec(memory_space=pltpu.VMEM)
    return pl.pallas_call(
        kernel,
        in_specs=[pl.BlockSpec(memory_space=pltpu.SMEM)] + [whole] * 6,
        out_specs=whole,
        scratch_shapes=[pltpu.VMEM((nx * 2 * LANES + 2 * EXTRA, deep), BF16)],
        out_shape=jax.ShapeDtypeStruct((nx, pieces, 2 * rows + EXTRA, LANES), BF16),
        compiler_params=pltpu.CompilerParams(vmem_limit_bytes=32 << 20),
        name="multiply",
    )(place, a, *blocks, came, jnp.asarray(turn), jnp.asarray(pick))


def finish(parts, row_code, col_code, q):
    nx, pieces, tall, _ = parts.shape
    rows = (tall - EXTRA) // 2
    ncol = col_code.shape[1]
    at, to = np.indices((EXTRA, 8))
    turn = onehot(at == to)

    def kernel(p_ref, turn_ref, r_ref, c_ref, o_ref, line):
        for p in range(pieces):
            total = p_ref[0, p].astype(F32)
            for x in range(1, nx):
                total = total + p_ref[x, p].astype(F32)
            last = dot(total[2 * rows :].astype(BF16), turn_ref[...], (0, 0))
            for parity in range(2):
                for half in range(2):
                    at = ((half * 2 + parity) * pieces + p) * q
                    own = slice(parity * rows, (parity + 1) * rows)
                    line[:, at : at + HALF] = total[own, half * HALF : (half + 1) * HALF]
                    col = parity * 2 + half
                    line[:LANES, at + HALF : at + q] = last[:, col : col + 1]
                    line[LANES:, at + HALF : at + q] = last[: rows - LANES, 4 + col : 5 + col]
        kept = r_ref[...] == c_ref[...]
        o_ref[...] = jnp.where(kept, line[...], 0.0).astype(BF16)

    return pl.pallas_call(
        kernel,
        out_shape=jax.ShapeDtypeStruct((rows, ncol), BF16),
        scratch_shapes=[pltpu.VMEM((rows, ncol), F32)],
        compiler_params=pltpu.CompilerParams(vmem_limit_bytes=32 << 20),
        name="finish",
    )(parts, jnp.asarray(turn), row_code, col_code)


def make_shards(ny, nx, nc):
    nzh, nzl = nx * nc * 2, 2
    nz = nzh * nzl
    swap = [(0, 1), (1, 0)]
    trade = [(s * nc + core, (s + (1 if s % 2 == core else -1)) % nz * nc + core) for s in range(nz) for core in range(nc)]

    def shards(amplitudes, integrals, occ_irrep, virt_irrep, slab_i, slab_j):
        vir, cblock = amplitudes.shape[1], amplitudes.shape[2]
        nk, q = integrals.shape[0], integrals.shape[2]
        ni = nzh * nzl
        na = vir // (ni * ny)
        zh, zl, y = lax.axis_index("zh"), lax.axis_index("zl"), lax.axis_index("y")
        x, c = lax.axis_index("x"), lax.axis_index("c")

        depth = -(-nk * cblock // LANES) * LANES
        w = pack_columns(integrals.transpose(2, 0, 1).reshape(q, nk * cblock))

        t = amplitudes.reshape(vir // na, na * cblock)
        t = lax.all_to_all(t, ("zh", "zl"), 0, 0, tiled=True)
        w = lax.all_gather(w, "zh", axis=0, tiled=True)
        t, w = lax.optimization_barrier((t, w))
        w = w.reshape(nx, nc, 2, SENT, LANES)
        t = lax.all_gather(t, ("y", "c"), axis=0, tiled=True)
        other = lax.ppermute(w, ("zh", "zl", "c"), trade)
        t, other = lax.optimization_barrier((t, other))
        given = [lax.dynamic_index_in_dim(part, 1 - c, 1, keepdims=False) for part in (w, other)]
        came = lax.ppermute(jnp.stack(given), "c", swap)
        t = order_rows(t, nk, nc, ny, ni, na, cblock, depth)

        parts = multiply(jnp.stack([zl, c]), t, [w, other], came)
        tall = parts.shape[2]
        parts = lax.all_to_all(parts.reshape(nx * ny * tall, LANES), ("x", "y"), 0, 0, tiled=True)
        parts = parts.reshape(nx, ny, tall, LANES)

        a_index = ((zh * nzl + zl) * ny + y) * na + jnp.arange(na, dtype=jnp.int32)
        irr_virt_rows = lookup(virt_irrep, a_index)
        irr_occ_rows = lookup(occ_irrep, slab_i)
        row_code = jnp.bitwise_xor(irr_virt_rows[:, None], irr_occ_rows[None, :]).reshape(na * ni, 1)
        ncol = 2 * nzl * ny * q
        col_index = (x * nc + c) * ncol + jnp.arange(ncol, dtype=jnp.int32)
        irr_occ_cols = lookup(lookup(occ_irrep, slab_j), col_index // vir)
        irr_virt_cols = lookup(virt_irrep, col_index % vir)
        col_code = jnp.bitwise_xor(irr_occ_cols, irr_virt_cols)[None, :]
        out = finish(parts, row_code, col_code, q)
        return out.reshape(na, ni, ncol).transpose(1, 0, 2)

    return shards


def solution(mesh):
    nx, nc, ny = 4, 2, 4
    fine = Mesh(mesh.devices.reshape(nx * nc * 2, 2, ny, nx, nc), ("zh", "zl", "y", "x", "c"))
    row, rep = ("zh", "zl", "y"), ("x", "c")
    return jax.shard_map(
        make_shards(ny, nx, nc),
        mesh=fine,
        in_specs=(P(row, None, rep), P(None, rep, row), P(), P(), P(), P()),
        out_specs=P(None, row, rep),
        check_vma=False,
    )
```

```python
import jax
import jax.numpy as jnp
import numpy as np
from jax import lax
from jax.experimental import pallas as pl
from jax.experimental.pallas import tpu as pltpu
from jax.sharding import Mesh, PartitionSpec as P

BF16 = jnp.bfloat16
F32 = jnp.float32
LANES = 128
HALF = 64
TAIL = 8
SENT = 160 + TAIL
EXTRA = 16


def lookup(table, index):
    compare = index[:, None] == jnp.arange(table.shape[0], dtype=jnp.int32)[None, :]
    return jnp.sum(jnp.where(compare, table[None, :], 0), axis=1)


def dot(a, b, contract):
    return lax.dot_general(a, b, ((contract[:1], contract[1:]), ((), ())), preferred_element_type=F32)


def onehot(hit):
    return np.asarray(hit).astype(np.dtype(jnp.bfloat16))


def order_rows(gathered, nk, nc, pieces, ni, na, cblock, depth):
    rows = ni * pieces
    to, at = np.indices((rows, rows))
    shuffle = onehot(at == to % ni * pieces + to // ni)

    def kernel(g_ref, s_ref, o_ref):
        blank = jnp.zeros((rows, depth - nk * cblock), F32)
        for core in range(nc):
            parts = []
            for k in range(nk):
                first = (k * nc + core) * rows
                parts.append(dot(s_ref[...], g_ref[first : first + rows, :], (1, 0)))
            for a in range(na):
                at = slice(a * cblock, (a + 1) * cblock)
                block = jnp.concatenate([part[:, at] for part in parts] + [blank], axis=1)
                block = block.astype(BF16).reshape(pieces, ni, depth)
                o_ref[:, a * ni : (a + 1) * ni, core * depth : (core + 1) * depth] = block

    return pl.pallas_call(
        kernel,
        out_shape=jax.ShapeDtypeStruct((pieces, na * ni, nc * depth), BF16),
        compiler_params=pltpu.CompilerParams(vmem_limit_bytes=32 << 20),
        name="order_rows",
    )(gathered, jnp.asarray(shuffle))


def pack_columns(w):
    fold = HALF // 2

    def kernel(w_ref, o_ref):
        w = w_ref[...].astype(F32)
        third = w[:HALF, 2 * LANES :]
        third = jnp.concatenate([third[:fold], third[fold:]], axis=1)
        end = w[HALF:, 2 * LANES :]
        last = [w[HALF:, :LANES], w[HALF:, LANES : 2 * LANES], jnp.concatenate([end, jnp.zeros_like(end)], axis=1)]
        last += [jnp.zeros((TAIL - 3, LANES), F32)]
        packed = [w[:HALF, :LANES], w[:HALF, LANES : 2 * LANES], third, jnp.concatenate(last, axis=0)]
        o_ref[...] = jnp.concatenate(packed, axis=0).astype(BF16)

    return pl.pallas_call(
        kernel,
        out_shape=jax.ShapeDtypeStruct((SENT, LANES), BF16),
        compiler_params=pltpu.CompilerParams(vmem_limit_bytes=32 << 20),
        name="pack_columns",
    )(w)


def multiply(place, a, blocks, came):
    pieces, rows, deep = a.shape
    nx, nc, halves = blocks[0].shape[:3]
    depth = deep // nc
    slots = nx * halves
    fold = HALF // 2
    to, at = np.indices((3 * EXTRA, slots * TAIL))
    turn = onehot((at % TAIL == to // EXTRA) & (at // TAIL == to % EXTRA))
    to, at = np.indices((nx * EXTRA, 4 * slots))
    x, part, parity, half = to // EXTRA, to % EXTRA // 4, to % 4 // 2, to % 2
    pick = onehot((to % EXTRA < 8) & (at == (part * 2 + parity) * slots + x * halves + half))

    def kernel(place_ref, a_ref, b0, b1, b2, turn_ref, pick_ref, o_ref, cols):
        for n in range(2 * nc):
            own_c, own_z = n // 2 == 0, n % 2 == 0
            block_of = lambda x, half, at: (b0, b1)[n % 2][x, place_ref[1], half, at, :] if own_c else b2[n % 2, x, half, at, :]
            parity = place_ref[0] if own_z else 1 - place_ref[0]
            core = place_ref[1] if own_c else 1 - place_ref[1]
            lanes = [pl.ds(pl.multiple_of(core * depth + tile * LANES, LANES), LANES) for tile in range(3)]
            for x in range(nx):
                for half in range(halves):
                    first = pl.multiple_of(((x * 2 + parity) * halves + half) * HALF, HALF)
                    for tile in range(2):
                        cols[pl.ds(first, HALF), lanes[tile]] = block_of(x, half, slice(tile * HALF, (tile + 1) * HALF))
                    third = block_of(x, half, slice(2 * HALF, 2 * HALF + fold)).astype(F32)
                    third = jnp.concatenate([third[:, :HALF], third[:, HALF:]], axis=0)
                    cols[pl.ds(first, HALF), lanes[2]] = jnp.concatenate([third, jnp.zeros_like(third)], axis=1).astype(BF16)
            last = [block_of(x, half, slice(SENT - TAIL, SENT)).astype(F32) for x in range(nx) for half in range(halves)]
            last = dot(turn_ref[...], jnp.concatenate(last, axis=0).astype(BF16), (1, 0)).astype(BF16)
            first = pl.multiple_of(nx * 2 * LANES + parity * EXTRA, EXTRA)
            for tile in range(3):
                cols[pl.ds(first, EXTRA), lanes[tile]] = last[tile * EXTRA : (tile + 1) * EXTRA]

        a = a_ref[...].reshape(pieces * rows, deep)
        for x in range(nx):
            out = dot(a, cols[x * 2 * LANES : (x + 1) * 2 * LANES, :], (1, 1)).astype(BF16)
            for p in range(pieces):
                for parity in range(2):
                    own = out[p * rows : (p + 1) * rows, parity * LANES : (parity + 1) * LANES]
                    o_ref[x, p, parity * rows : (parity + 1) * rows, :] = own
        blank = jnp.zeros((slots, 2 * LANES - rows), F32)
        every = dot(a, cols[nx * 2 * LANES :, :], (1, 1))
        for p in range(pieces):
            last = every[p * rows : (p + 1) * rows].T
            left = [last[at * EXTRA : at * EXTRA + slots] for at in range(2)]
            left = [part[:, :LANES] for part in left] + [jnp.concatenate([part[:, LANES:], blank], axis=1) for part in left]
            left = dot(pick_ref[...], jnp.concatenate(left, axis=0).astype(BF16), (1, 0)).astype(BF16)
            for x in range(nx):
                o_ref[x, p, 2 * rows :, :] = left[x * EXTRA : (x + 1) * EXTRA]

    whole = pl.BlockSpec(memory_space=pltpu.VMEM)
    return pl.pallas_call(
        kernel,
        in_specs=[pl.BlockSpec(memory_space=pltpu.SMEM)] + [whole] * 6,
        out_specs=whole,
        scratch_shapes=[pltpu.VMEM((nx * 2 * LANES + 2 * EXTRA, deep), BF16)],
        out_shape=jax.ShapeDtypeStruct((nx, pieces, 2 * rows + EXTRA, LANES), BF16),
        compiler_params=pltpu.CompilerParams(vmem_limit_bytes=32 << 20),
        name="multiply",
    )(place, a, *blocks, came, jnp.asarray(turn), jnp.asarray(pick))


def finish(parts, row_code, col_code, q):
    nx, pieces, tall, _ = parts.shape
    rows = (tall - EXTRA) // 2
    ncol = col_code.shape[1]
    at, to = np.indices((EXTRA, 8))
    turn = onehot(at == to)

    def kernel(p_ref, turn_ref, r_ref, c_ref, o_ref, line):
        for p in range(pieces):
            total = p_ref[0, p].astype(F32)
            for x in range(1, nx):
                total = total + p_ref[x, p].astype(F32)
            last = dot(total[2 * rows :].astype(BF16), turn_ref[...], (0, 0))
            for parity in range(2):
                for half in range(2):
                    at = ((half * 2 + parity) * pieces + p) * q
                    own = slice(parity * rows, (parity + 1) * rows)
                    line[:, at : at + HALF] = total[own, half * HALF : (half + 1) * HALF]
                    col = parity * 2 + half
                    line[:LANES, at + HALF : at + q] = last[:, col : col + 1]
                    line[LANES:, at + HALF : at + q] = last[: rows - LANES, 4 + col : 5 + col]
        kept = r_ref[...] == c_ref[...]
        o_ref[...] = jnp.where(kept, line[...], 0.0).astype(BF16)

    return pl.pallas_call(
        kernel,
        out_shape=jax.ShapeDtypeStruct((rows, ncol), BF16),
        scratch_shapes=[pltpu.VMEM((rows, ncol), F32)],
        compiler_params=pltpu.CompilerParams(vmem_limit_bytes=32 << 20),
        name="finish",
    )(parts, jnp.asarray(turn), row_code, col_code)


def make_shards(ny, nx, nc):
    nzh, nzl = nx * nc * 2, 2
    nz = nzh * nzl
    swap = [(0, 1), (1, 0)]
    trade = [(s * nc + core, (s + (1 if s % 2 == core else -1)) % nz * nc + core) for s in range(nz) for core in range(nc)]

    def shards(amplitudes, integrals, occ_irrep, virt_irrep, slab_i, slab_j):
        vir, cblock = amplitudes.shape[1], amplitudes.shape[2]
        nk, q = integrals.shape[0], integrals.shape[2]
        ni = nzh * nzl
        na = vir // (ni * ny)
        zh, zl, y = lax.axis_index("zh"), lax.axis_index("zl"), lax.axis_index("y")
        x, c = lax.axis_index("x"), lax.axis_index("c")

        depth = -(-nk * cblock // LANES) * LANES
        w = pack_columns(integrals.transpose(2, 0, 1).reshape(q, nk * cblock))

        t = amplitudes.reshape(vir // na, na * cblock)
        t = lax.all_to_all(t, ("zh", "zl"), 0, 0, tiled=True)
        w = lax.all_gather(w, "zh", axis=0, tiled=True)
        t, w = lax.optimization_barrier((t, w))
        w = w.reshape(nx, nc, 2, SENT, LANES)
        t = lax.all_gather(t, ("y", "c"), axis=0, tiled=True)
        other = lax.ppermute(w, ("zh", "zl", "c"), trade)
        t, other = lax.optimization_barrier((t, other))
        given = [lax.dynamic_index_in_dim(part, 1 - c, 1, keepdims=False) for part in (w, other)]
        came = lax.ppermute(jnp.stack(given), "c", swap)
        t = order_rows(t, nk, nc, ny, ni, na, cblock, depth)

        parts = multiply(jnp.stack([zl, c]), t, [w, other], came)
        tall = parts.shape[2]
        parts = lax.all_to_all(parts.reshape(nx * ny * tall, LANES), ("x", "y"), 0, 0, tiled=True)
        parts = parts.reshape(nx, ny, tall, LANES)

        a_index = ((zh * nzl + zl) * ny + y) * na + jnp.arange(na, dtype=jnp.int32)
        irr_virt_rows = lookup(virt_irrep, a_index)
        irr_occ_rows = lookup(occ_irrep, slab_i)
        row_code = jnp.bitwise_xor(irr_virt_rows[:, None], irr_occ_rows[None, :]).reshape(na * ni, 1)
        ncol = 2 * nzl * ny * q
        col_index = (x * nc + c) * ncol + jnp.arange(ncol, dtype=jnp.int32)
        irr_occ_cols = lookup(lookup(occ_irrep, slab_j), col_index // vir)
        irr_virt_cols = lookup(virt_irrep, col_index % vir)
        col_code = jnp.bitwise_xor(irr_occ_cols, irr_virt_cols)[None, :]
        out = finish(parts, row_code, col_code, q)
        return out.reshape(na, ni, ncol).transpose(1, 0, 2)

    return shards


def solution(mesh):
    nx, nc, ny = 4, 2, 4
    fine = Mesh(mesh.devices.reshape(nx * nc * 2, 2, ny, nx, nc), ("zh", "zl", "y", "x", "c"))
    row, rep = ("zh", "zl", "y"), ("x", "c")
    return jax.shard_map(
        make_shards(ny, nx, nc),
        mesh=fine,
        in_specs=(P(row, None, rep), P(None, rep, row), P(), P(), P(), P()),
        out_specs=P(None, row, rep),
        check_vma=False,
    )
```
